32 devices in a mesh: groups: 2 (over y), row: 4 (over z), chan: 2 (over x), sub: 2 (over core).
Axes of the slice: x: 2, y: 2, z: 4, core: 2. Of those that a mesh axis runs over, the one named last changes fastest.
Arguments:
- pair: bfloat16 [64, 32, 128], P(('groups', 'row'), ('chan', 'sub')), parts along dimension 0, may hold values from -8 to 8
- cotangent: bfloat16 [64, 32, 128], P(('groups', 'row'), ('chan', 'sub')), parts along dimension 0, may hold values from -6 to 6
- token_mask: int32 [64], P('groups'), parts along dimension 0, may hold values 0 or 1
- w_in: bfloat16 [2, 128, 640], replicated, may hold values from -0.5 to 0.5
- w_out: bfloat16 [2, 128, 128], replicated, may hold values from -0.5 to 0.5
Outputs:
- updated: bfloat16 [64, 32, 128], P(('groups', 'row'), ('chan', 'sub')), parts along dimension 0
- pair_grad: bfloat16 [64, 32, 128], P(('groups', 'row'), ('chan', 'sub')), parts along dimension 0
- grad_w_in: float32 [4, 128, 640], P('groups'), parts along dimension 0
- grad_w_out: float32 [4, 128, 128], P('groups'), parts along dimension 0
The draws below stay inside these ranges and needn't reach their ends.
There are 2 independent parts, one for each index of `groups`. The reference program is written for one: setup_inputs(seed, part) draws one part's arguments, and reference() takes and returns one part's arrays. A program takes and returns all parts, laid end to end along the dimension named above; an argument that names none is the same for every part. Nothing has to cross between parts.
All inputs are finite; a program needn't handle non-finite values.
Results may differ from the reference program's by a relative error of at most 0.013.
Values may be sent and summed in bfloat16 or wider, within the bound.
No kernel may reach another device: no remote copies, remote signals or barrier semaphores. Data moves between devices by JAX's collectives and lax.ppermute only.
A program may use at most 64 MiB of HBM per device.

```python
import jax
import jax.numpy as jnp
from jax import lax

CZ = 128
CH = 128
ROWS_DEV = 8
TOKENS = 32
N_ROW = 4


def draw_pair(key, part):
    key = jax.random.fold_in(key, 11)
    key_noise, key_scale = jax.random.split(key, 2)
    randoms = jax.random.normal(key_noise, (TOKENS, TOKENS, CZ), jnp.float32)
    scales = jnp.exp(jax.random.uniform(key_scale, (CZ,), jnp.float32, -1.15, 1.15))
    values = randoms * scales
    return jnp.clip(values, -8.0, 8.0).astype(jnp.bfloat16)


def touch_ends(entries, rng, low, high):
    longest = entries.shape.index(max(entries.shape))
    spots = []
    for shift in (0, 1):
        where = [jax.random.randint(jax.random.fold_in(rng, axis), (), 0, length) for axis, length in enumerate(entries.shape)]
        where[longest] = (where[longest] + shift) % entries.shape[longest]
        spots.append(tuple(where))
    return entries.at[spots[0]].set(low).at[spots[1]].set(high)


def steps_of(rng, extent, cuts, smallest, high):
    def one(position, parts):
        heights = jax.random.uniform(jax.random.fold_in(jax.random.fold_in(rng, 6), position), (parts,), jnp.float32, smallest / len(cuts), high / len(cuts))
        return jnp.repeat(jnp.exp(heights), extent[position] // parts).reshape((-1,) + (1,) * (len(extent) - position - 1))

    gain = one(*cuts[0])
    for cut in cuts[1:]:
        gain = gain * one(*cut)
    return gain


def centred(stream_key, dims, deviation, bound, cuts=(), dtype=jnp.bfloat16):
    factor_of = steps_of(stream_key, dims, cuts, -0.22, 0.18) if cuts else 1.0
    result = jax.random.normal(stream_key, dims, jnp.float32) * deviation * factor_of
    return jnp.minimum(jnp.maximum(result, -bound), bound).astype(dtype)


def setup_inputs(seed: int = 0, part: int = 0) -> dict:
    key_of = jax.random.split(jax.random.key(seed), 6)
    own_keys = jax.random.split(jax.random.fold_in(key_of[5], part), 6)
    pair = draw_pair(jax.random.fold_in(jax.random.fold_in(key_of[5], part), 71), part)
    cotangent = centred(own_keys[1], (TOKENS, TOKENS, CZ), 1.0, 6.0, ((0, 4), (1, 4)))
    token_mask = touch_ends((jax.random.randint(own_keys[2], (TOKENS,), 0, 8) < 7).astype(jnp.int32), jax.random.fold_in(own_keys[2], 1), 0, 1)
    w_in = centred(key_of[3], (2, CZ, 4 * CH + CZ), CZ ** -0.5, 0.5)
    w_out = centred(key_of[4], (2, CH, CZ), CH ** -0.5, 0.5)
    return dict(pair=pair, cotangent=cotangent, token_mask=token_mask, w_in=w_in, w_out=w_out)


EPSILON = 1e-05
ACCURATE = lax.Precision.HIGHEST

def layer_norm(values, norm_axis):
    centre = lax.optimization_barrier(jnp.mean(values, axis=norm_axis, keepdims=True))
    shifted = values - centre
    spread = lax.optimization_barrier(jnp.mean(shifted * shifted, axis=norm_axis, keepdims=True))
    inverse = lax.rsqrt(spread + EPSILON)
    return (shifted * inverse, inverse)

def norm_grad(upstream, normed, inverse, norm_axis):
    return inverse * (upstream - lax.optimization_barrier(jnp.mean(upstream, axis=norm_axis, keepdims=True)) - normed * lax.optimization_barrier(jnp.mean(upstream * normed, axis=norm_axis, keepdims=True)))

def product_of(pattern, left_op, right_op):
    return jnp.einsum(pattern, left_op.astype(jnp.float32), right_op.astype(jnp.float32), precision=ACCURATE)

def split_weights(w_in_u, hidden):
    channels = w_in_u.shape[0]
    return (w_in_u[:, :4 * hidden].reshape(channels, 4, hidden), w_in_u[:, 4 * hidden:])

def front_block(state_block, rows_mask, cols_mask, w_in_u, hidden):
    normed, _ = layer_norm(state_block.astype(jnp.float32), -1)
    normed = normed.astype(jnp.bfloat16)
    w_pairs, w_gate = split_weights(w_in_u, hidden)
    projected = product_of('rjc,cke->kerj', normed, w_pairs)
    pair_mask = rows_mask[:, None] * cols_mask[None, :]
    left_side = jax.nn.sigmoid(projected[1]) * projected[0] * pair_mask
    right_side = jax.nn.sigmoid(projected[3]) * projected[2] * pair_mask
    return jnp.stack([left_side, right_side]).astype(jnp.bfloat16)

def back_block(state_block, tri_block, w_in_u, w_out_u, hidden):
    normed, _ = layer_norm(state_block.astype(jnp.float32), -1)
    normed = normed.astype(jnp.bfloat16)
    _, w_gate = split_weights(w_in_u, hidden)
    gate_value = jax.nn.sigmoid(product_of('rjc,cd->rjd', normed, w_gate))
    tnorm, _ = layer_norm(tri_block.astype(jnp.float32), 0)
    linear = product_of('erj,ec->rjc', tnorm.astype(jnp.bfloat16), w_out_u)
    return (state_block.astype(jnp.float32) + gate_value * linear).astype(jnp.bfloat16)

def grad_back_block(state_block, tri_block, upstream, w_in_u, w_out_u, hidden):
    normed, _ = layer_norm(state_block.astype(jnp.float32), -1)
    normed = normed.astype(jnp.bfloat16)
    _, w_gate = split_weights(w_in_u, hidden)
    gate_value = jax.nn.sigmoid(product_of('rjc,cd->rjd', normed, w_gate))
    tnorm, inverse = layer_norm(tri_block.astype(jnp.float32), 0)
    tnorm_low = tnorm.astype(jnp.bfloat16)
    grad_hidden = (upstream * gate_value).astype(jnp.bfloat16)
    wo_term = product_of('erj,rjc->ec', tnorm_low, grad_hidden)
    grad_tn = product_of('rjc,ec->erj', grad_hidden, w_out_u)
    grad_tri = norm_grad(grad_tn, tnorm, inverse, 0).astype(jnp.bfloat16)
    return (grad_tri, wo_term)

def grad_front_block(state_block, tri_block, grad_pairs, upstream, rows_mask, cols_mask, w_in_u, w_out_u, hidden):
    normed_full, inverse = layer_norm(state_block.astype(jnp.float32), -1)
    normed = normed_full.astype(jnp.bfloat16)
    w_pairs, w_gate = split_weights(w_in_u, hidden)
    projected = product_of('rjc,cke->kerj', normed, w_pairs)
    gate_value = jax.nn.sigmoid(product_of('rjc,cd->rjd', normed, w_gate))
    tnorm, _ = layer_norm(tri_block.astype(jnp.float32), 0)
    linear = product_of('erj,ec->rjc', tnorm.astype(jnp.bfloat16), w_out_u)
    grad_gate = (upstream * linear * gate_value * (1.0 - gate_value)).astype(jnp.bfloat16)
    pair_mask = rows_mask[:, None] * cols_mask[None, :]
    sig_left = jax.nn.sigmoid(projected[1])
    sig_right = jax.nn.sigmoid(projected[3])
    grad_left = grad_pairs[0].astype(jnp.float32) * pair_mask
    grad_right = grad_pairs[1].astype(jnp.float32) * pair_mask
    grad_proj = jnp.stack([grad_left * sig_left, grad_left * projected[0] * sig_left * (1.0 - sig_left), grad_right * sig_right, grad_right * projected[2] * sig_right * (1.0 - sig_right)]).astype(jnp.bfloat16)
    channels = state_block.shape[2]
    pair_term = product_of('rjc,kerj->cke', normed, grad_proj).reshape(channels, 4 * hidden)
    gate_term = product_of('rjc,rjd->cd', normed, grad_gate)
    wi_term = jnp.concatenate([pair_term, gate_term], axis=1)
    grad_normed = product_of('kerj,cke->rjc', grad_proj, w_pairs) + product_of('rjd,cd->rjc', grad_gate, w_gate)
    grad_x = upstream + norm_grad(grad_normed, normed_full, inverse, -1)
    return (grad_x, wi_term)

def triangle(pairs, incoming):

    def one_channel(operands):
        left_mat = operands[0].astype(jnp.float32)
        right_mat = operands[1].astype(jnp.float32)
        if incoming:
            return jnp.dot(left_mat.T, right_mat, precision=ACCURATE)
        return jnp.dot(left_mat, right_mat.T, precision=ACCURATE)
    return lax.map(one_channel, (pairs[0], pairs[1])).astype(jnp.bfloat16)

def triangle_grad(pairs, grad_tri, incoming):

    def one_channel(operands):
        left_mat = operands[0].astype(jnp.float32)
        right_mat = operands[1].astype(jnp.float32)
        grad_mat = operands[2].astype(jnp.float32)
        if incoming:
            return jnp.stack([jnp.dot(right_mat, grad_mat.T, precision=ACCURATE), jnp.dot(left_mat, grad_mat, precision=ACCURATE)])
        return jnp.stack([jnp.dot(grad_mat, right_mat, precision=ACCURATE), jnp.dot(grad_mat.T, left_mat, precision=ACCURATE)])
    stacked = lax.map(one_channel, (pairs[0], pairs[1], grad_tri))
    return jnp.moveaxis(stacked, 1, 0).astype(jnp.bfloat16)

def reference(pair, cotangent, token_mask, w_in, w_out):
    hidden = w_out.shape[1]
    mask_full = token_mask.astype(jnp.float32)
    mask_blocks = mask_full.reshape(N_ROW, ROWS_DEV)
    states = [pair]
    saved = []
    for layer_id in range(2):
        state_blocks = states[-1].reshape(N_ROW, ROWS_DEV, TOKENS, CZ)
        fronted = lax.map(lambda operands: front_block(operands[0], operands[1], mask_full, w_in[layer_id], hidden), (state_blocks, mask_blocks))
        pairs = fronted.transpose(1, 2, 0, 3, 4).reshape(2, hidden, TOKENS, TOKENS)
        triangles = triangle(pairs, layer_id == 1)
        tri_blocks = triangles.reshape(hidden, N_ROW, ROWS_DEV, TOKENS).transpose(1, 0, 2, 3)
        stepped = lax.map(lambda operands: back_block(operands[0], operands[1], w_in[layer_id], w_out[layer_id], hidden), (state_blocks, tri_blocks))
        states.append(stepped.reshape(TOKENS, TOKENS, CZ))
        saved.append((pairs, tri_blocks))
    upstream = cotangent.astype(jnp.float32)
    wi_grads = [None, None]
    wo_grads = [None, None]
    for layer_id in (1, 0):
        pairs, tri_blocks = saved[layer_id]
        state_blocks = states[layer_id].reshape(N_ROW, ROWS_DEV, TOKENS, CZ)
        up_blocks = upstream.reshape(N_ROW, ROWS_DEV, TOKENS, CZ)
        grad_tri_blocks, wo_terms = lax.map(lambda operands: grad_back_block(operands[0], operands[1], operands[2], w_in[layer_id], w_out[layer_id], hidden), (state_blocks, tri_blocks, up_blocks))
        grad_tri = grad_tri_blocks.transpose(1, 0, 2, 3).reshape(hidden, TOKENS, TOKENS)
        grad_pairs = triangle_grad(pairs, grad_tri, layer_id == 1)
        pair_blocks = grad_pairs.reshape(2, hidden, N_ROW, ROWS_DEV, TOKENS).transpose(2, 0, 1, 3, 4)
        grad_blocks, wi_terms = lax.map(lambda operands: grad_front_block(operands[0], operands[1], operands[2], operands[3], operands[4], mask_full, w_in[layer_id], w_out[layer_id], hidden), (state_blocks, tri_blocks, pair_blocks, up_blocks, mask_blocks))
        upstream = grad_blocks.reshape(TOKENS, TOKENS, CZ)
        wi_grads[layer_id] = lax.optimization_barrier(jnp.sum(wi_terms, axis=0)) / TOKENS
        wo_grads[layer_id] = lax.optimization_barrier(jnp.sum(wo_terms, axis=0)) / TOKENS
    return (states[2], upstream.astype(jnp.bfloat16), jnp.stack(wi_grads), jnp.stack(wo_grads))
```

```python
import functools

import jax
import jax.numpy as jnp
from jax import lax
from jax.experimental import pallas as pl
from jax.experimental.pallas import tpu as pltpu
from jax.sharding import PartitionSpec as P

EPSILON = 1e-05
F32 = jnp.float32
BF16 = jnp.bfloat16
TILE = 8
PLANES = 40
VMEM_BYTES = 56 * 2**20
VMEM_PLAN = 40 * 2**20


def dot(left, right):
    return lax.dot_general(left, right, (((1,), (0,)), ((), ())), preferred_element_type=F32)


def dot_rows(left, right):
    return lax.dot_general(left, right, (((0,), (0,)), ((), ())), preferred_element_type=F32)


def dot_last(left, right):
    return lax.dot_general(left, right, (((1,), (1,)), ((), ())), preferred_element_type=F32)


def lane_mean(values):
    return jnp.mean(values, axis=-1, keepdims=True)


def norm_of(values):
    shifted = values - lane_mean(values)
    inverse = lax.rsqrt(lane_mean(shifted * shifted) + EPSILON)
    return shifted * inverse, inverse


def norm_back(upstream, normed, inverse):
    return inverse * (upstream - lane_mean(upstream) - normed * lane_mean(upstream * normed))


def sigmoid(values):
    return 0.5 * jnp.tanh(0.5 * values) + 0.5


def rounded(values):
    return values.astype(BF16).astype(F32)


def triangle(tokens, left, left_row, right, right_turned, store, group):
    tiles = tokens // TILE

    def right_tile(r, q):
        if right_turned:
            return right[pl.ds(q * TILE * tokens + r, TILE, stride=tokens), :]
        return right[pl.ds(r * tokens + q * TILE, TILE), :]

    def body(step, carry):
        first = step * group
        totals = [[None] * tiles for _ in range(group)]
        for r in range(tokens):
            column = [right_tile(r, q) for q in range(tiles)]
            for g in range(group):
                scale = jnp.broadcast_to(left[pl.ds(left_row(first + g, r), 1), :], column[0].shape)
                for q in range(tiles):
                    term = scale * column[q]
                    totals[g][q] = term if r == 0 else totals[g][q] + term
        for g in range(group):
            store(first + g, totals[g])
        return carry

    lax.fori_loop(0, tokens // group, body, 0)


def whole_kernel(
    tokens, sizes, chunk, group, parts_ref, mask_ref, w_in_ref, w_out_ref,
    updated_ref, pair_grad_ref, gwi_ref, gwo_ref,
    states, cot, flat, side, normed, inv, normed16, one_a, two_a, one_b, two_b, gate, tnorm, tinv, tnorm16, linear,
    tri, ga, gb, w_turned, wo_turned, gproj,
):
    n_row, n_chan, n_sub = sizes
    row_id, chan_id, sub_id = lax.axis_index("row"), lax.axis_index("chan"), lax.axis_index("sub")
    rows, cols = tokens // n_row, tokens // (n_chan * n_sub)
    pairs = tokens * tokens
    hidden = w_out_ref.shape[1]
    channels = w_in_ref.shape[1]
    steps = pairs // chunk
    x_ref, gy_ref = states.at[0], cot

    for s_row in range(n_row):
        for s_chan in range(n_chan):
            for s_sub in range(n_sub):
                r0 = lax.rem(row_id + n_row - s_row, n_row) * rows
                c0 = (lax.rem(chan_id + n_chan - s_chan, n_chan) * n_sub + lax.rem(sub_id + n_sub - s_sub, n_sub)) * cols
                c0 = pl.multiple_of(c0, TILE)
                for which, target in ((0, x_ref), (1, gy_ref)):
                    block = parts_ref[s_row, s_chan, s_sub, which].astype(F32).reshape(rows, cols, channels)
                    for r in range(rows):
                        at = pl.multiple_of((r0 + r) * tokens + c0, TILE)
                        target[pl.ds(at, cols), :] = block[r]

    for u in range(2):
        w_turned[u] = w_in_ref[u].T
        wo_turned[u] = w_out_ref[u].T

    def mask_of(step):
        lines = chunk // tokens
        outer = mask_ref[pl.ds(pl.multiple_of(step * lines, lines), lines), :]
        full = mask_ref[...]
        return (outer[:, None, :] * full[None, :, :]).reshape(chunk, channels)

    def at_chunk(step):
        return pl.ds(pl.multiple_of(step * chunk, chunk), chunk)

    def front(u, x, step):
        here = at_chunk(step)
        n, s = norm_of(x)
        normed[u, here, :] = n
        inv[u, here, :] = jnp.broadcast_to(s, n.shape)
        n16 = n.astype(BF16)
        normed16[u, here, :] = n16
        projected = dot(n16, w_in_ref[u])
        pa, qa, pb, qb, qz = [projected[:, hidden * k : hidden * (k + 1)] for k in range(5)]
        mask = mask_of(step)
        for p, q, one, two, keep in ((pa, qa, one_a, two_a, flat), (pb, qb, one_b, two_b, side)):
            sig = sigmoid(q)
            first = sig * mask
            value = first * p
            one[u, here, :] = first
            two[u, here, :] = value * (1.0 - sig)
            keep[u, here, :] = rounded(value)
        gate[u, here, :] = sigmoid(qz)

    def back(u, step):
        here = at_chunk(step)
        tn, r = norm_of(rounded(tri[here, :]))
        tnorm[u, here, :] = tn
        tinv[u, here, :] = jnp.broadcast_to(r, tn.shape)
        tn16 = tn.astype(BF16)
        tnorm16[u, here, :] = tn16
        lin = dot(tn16, w_out_ref[u])
        linear[u, here, :] = lin
        return rounded(states[u, here, :] + gate[u, here, :] * lin)

    def grad_back(u, gy, step):
        here = at_chunk(step)
        gh = (gy * gate[u, here, :]).astype(BF16)
        term = dot_rows(tnorm16[u, here, :], gh)
        gwo_ref[u] = gwo_ref[u] + term
        gtn = dot(gh, wo_turned[u])
        tri[here, :] = rounded(norm_back(gtn, tnorm[u, here, :], tinv[u, here, :]))

    def grad_front(u, gy, step, wants_all):
        here = at_chunk(step)
        z = gate[u, here, :]
        ga16 = rounded(ga[here, :])
        gb16 = rounded(gb[here, :])
        pieces = [
            ga16 * one_a[u, here, :],
            ga16 * two_a[u, here, :],
            gb16 * one_b[u, here, :],
            gb16 * two_b[u, here, :],
            gy * linear[u, here, :] * z * (1.0 - z),
        ]
        g = jnp.concatenate([p.astype(BF16) for p in pieces], axis=1)
        gwi_ref[u] = gwi_ref[u] + dot_rows(normed16[u, here, :], g)
        if not wants_all:
            return None
        h = dot(g, w_turned[u])
        return gy + norm_back(h, normed[u, here, :], inv[u, here, :])

    def loop(body):
        def step_of(step, carry):
            body(step)
            return carry

        lax.fori_loop(0, steps, step_of, 0)

    def store_to(target):
        def store(p, values):
            for q, value in enumerate(values):
                target[pl.ds(pl.multiple_of(p * tokens + q * TILE, TILE), TILE), :] = value

        return store

    natural = lambda p, r: p * tokens + r
    turned = lambda p, r: r * tokens + p

    gwi_ref[...] = jnp.zeros(gwi_ref.shape, F32)
    gwo_ref[...] = jnp.zeros(gwo_ref.shape, F32)

    loop(lambda step: front(0, states[0, at_chunk(step), :], step))
    triangle(tokens, flat.at[0], natural, side.at[0], True, store_to(tri), group)

    def middle(step):
        x1 = back(0, step)
        states[1, at_chunk(step), :] = x1
        front(1, x1, step)

    loop(middle)
    triangle(tokens, flat.at[1], turned, side.at[1], False, store_to(tri), group)

    def turn(step):
        states[0, at_chunk(step), :] = back(1, step)
        grad_back(1, gy_ref[at_chunk(step), :], step)

    loop(turn)

    triangle(tokens, side.at[1], natural, tri, True, store_to(ga), group)
    triangle(tokens, flat.at[1], natural, tri, False, store_to(gb), group)

    def down(step):
        gx = grad_front(1, gy_ref[at_chunk(step), :], step, True)
        gy_ref[at_chunk(step), :] = gx
        grad_back(0, gx, step)

    loop(down)
    triangle(tokens, tri, natural, side.at[0], False, store_to(ga), group)
    triangle(tokens, tri, turned, flat.at[0], False, store_to(gb), group)

    def last(step):
        gx = grad_front(0, gy_ref[at_chunk(step), :], step, True)
        gy_ref[at_chunk(step), :] = gx

    loop(last)
    gwi_ref[...] = gwi_ref[...] * (1.0 / tokens)
    gwo_ref[...] = gwo_ref[...] * (1.0 / tokens)

    r0 = row_id * rows
    c0 = pl.multiple_of((chan_id * n_sub + sub_id) * cols, TILE)
    for source, target in ((states.at[0], updated_ref), (gy_ref, pair_grad_ref)):
        for r in range(rows):
            at = pl.multiple_of((r0 + r) * tokens + c0, TILE)
            target[r] = source[pl.ds(at, cols), :].astype(BF16)


def gather_part(pair, cotangent, sizes):
    channels = pair.shape[-1]
    block = jnp.stack([pair.reshape(-1, channels), cotangent.reshape(-1, channels)])
    for axis, size in zip(("sub", "chan", "row"), sizes[::-1]):
        moved = [block]
        for shift in range(1, size):
            moved.append(lax.ppermute(block, axis, [(i, (i + shift) % size) for i in range(size)]))
        block = jnp.stack(moved)
    return block


def whole_part(sizes, pair, cotangent, token_mask, w_in, w_out):
    tokens = token_mask.shape[0]
    channels = pair.shape[-1]
    hidden = w_out.shape[1]
    pairs = tokens * tokens
    parts = gather_part(pair, cotangent, sizes)
    mask = jnp.broadcast_to(token_mask.astype(F32)[:, None], (tokens, channels))
    chunk = 8 * tokens
    plane = pltpu.VMEM((pairs, channels), F32)
    two = pltpu.VMEM((2, pairs, channels), F32)
    two16 = pltpu.VMEM((2, pairs, channels), BF16)
    vmem = pl.BlockSpec(memory_space=pltpu.VMEM)
    return pl.pallas_call(
        functools.partial(whole_kernel, tokens, sizes, chunk, 8),
        out_shape=(
            jax.ShapeDtypeStruct(pair.shape, BF16),
            jax.ShapeDtypeStruct(pair.shape, BF16),
            jax.ShapeDtypeStruct(w_in.shape, F32),
            jax.ShapeDtypeStruct(w_out.shape, F32),
        ),
        in_specs=[vmem] * 4,
        out_specs=(vmem,) * 4,
        scratch_shapes=[
            two, plane, two, two, two, two, two16, two, two, two, two, two, two, two, two16, two,
            plane, plane, plane,
            pltpu.VMEM((2, w_in.shape[2], channels), BF16),
            pltpu.VMEM((2, channels, hidden), BF16),
            pltpu.VMEM((chunk, w_in.shape[2]), BF16),
        ],
        compiler_params=pltpu.CompilerParams(vmem_limit_bytes=VMEM_BYTES),
    )(parts, mask, w_in, w_out)


def layer_norm(values, norm_axis):
    centre = jnp.mean(values, axis=norm_axis, keepdims=True)
    shifted = values - centre
    spread = jnp.mean(shifted * shifted, axis=norm_axis, keepdims=True)
    inverse = lax.rsqrt(spread + EPSILON)
    return (shifted * inverse, inverse)


def norm_grad(upstream, normed, inverse, norm_axis):
    return inverse * (
        upstream
        - jnp.mean(upstream, axis=norm_axis, keepdims=True)
        - normed * jnp.mean(upstream * normed, axis=norm_axis, keepdims=True)
    )


def product_of(pattern, left_op, right_op):
    return jnp.einsum(pattern, left_op, right_op, preferred_element_type=jnp.float32)


def split_weights(w_in_u, hidden):
    channels = w_in_u.shape[0]
    return (w_in_u[:, : 4 * hidden].reshape(channels, 4, hidden), w_in_u[:, 4 * hidden :])


def front_block(state_block, rows_mask, cols_mask, w_in_u, hidden):
    normed, _ = layer_norm(state_block.astype(jnp.float32), -1)
    normed = normed.astype(jnp.bfloat16)
    w_pairs, w_gate = split_weights(w_in_u, hidden)
    projected = product_of("rjc,cke->kerj", normed, w_pairs)
    pair_mask = rows_mask[:, None] * cols_mask[None, :]
    left_side = jax.nn.sigmoid(projected[1]) * projected[0] * pair_mask
    right_side = jax.nn.sigmoid(projected[3]) * projected[2] * pair_mask
    return jnp.stack([left_side, right_side]).astype(jnp.bfloat16)


def back_block(state_block, tri_block, w_in_u, w_out_u, hidden):
    normed, _ = layer_norm(state_block.astype(jnp.float32), -1)
    normed = normed.astype(jnp.bfloat16)
    _, w_gate = split_weights(w_in_u, hidden)
    gate_value = jax.nn.sigmoid(product_of("rjc,cd->rjd", normed, w_gate))
    tnorm, _ = layer_norm(tri_block.astype(jnp.float32), 0)
    linear = product_of("erj,ec->rjc", tnorm.astype(jnp.bfloat16), w_out_u)
    return (state_block.astype(jnp.float32) + gate_value * linear).astype(jnp.bfloat16)


def grad_back_block(state_block, tri_block, upstream, w_in_u, w_out_u, hidden):
    normed, _ = layer_norm(state_block.astype(jnp.float32), -1)
    normed = normed.astype(jnp.bfloat16)
    _, w_gate = split_weights(w_in_u, hidden)
    gate_value = jax.nn.sigmoid(product_of("rjc,cd->rjd", normed, w_gate))
    tnorm, inverse = layer_norm(tri_block.astype(jnp.float32), 0)
    tnorm_low = tnorm.astype(jnp.bfloat16)
    grad_hidden = (upstream * gate_value).astype(jnp.bfloat16)
    wo_term = product_of("erj,rjc->ec", tnorm_low, grad_hidden)
    grad_tn = product_of("rjc,ec->erj", grad_hidden, w_out_u)
    grad_tri = norm_grad(grad_tn, tnorm, inverse, 0).astype(jnp.bfloat16)
    return (grad_tri, wo_term)


def grad_front_block(
    state_block, tri_block, grad_pairs, upstream, rows_mask, cols_mask, w_in_u, w_out_u, hidden
):
    normed_full, inverse = layer_norm(state_block.astype(jnp.float32), -1)
    normed = normed_full.astype(jnp.bfloat16)
    w_pairs, w_gate = split_weights(w_in_u, hidden)
    projected = product_of("rjc,cke->kerj", normed, w_pairs)
    gate_value = jax.nn.sigmoid(product_of("rjc,cd->rjd", normed, w_gate))
    tnorm, _ = layer_norm(tri_block.astype(jnp.float32), 0)
    linear = product_of("erj,ec->rjc", tnorm.astype(jnp.bfloat16), w_out_u)
    grad_gate = (upstream * linear * gate_value * (1.0 - gate_value)).astype(jnp.bfloat16)
    pair_mask = rows_mask[:, None] * cols_mask[None, :]
    sig_left = jax.nn.sigmoid(projected[1])
    sig_right = jax.nn.sigmoid(projected[3])
    grad_left = grad_pairs[0].astype(jnp.float32) * pair_mask
    grad_right = grad_pairs[1].astype(jnp.float32) * pair_mask
    grad_proj = jnp.stack(
        [
            grad_left * sig_left,
            grad_left * projected[0] * sig_left * (1.0 - sig_left),
            grad_right * sig_right,
            grad_right * projected[2] * sig_right * (1.0 - sig_right),
        ]
    ).astype(jnp.bfloat16)
    channels = state_block.shape[2]
    pair_term = product_of("rjc,kerj->cke", normed, grad_proj).reshape(channels, 4 * hidden)
    gate_term = product_of("rjc,rjd->cd", normed, grad_gate)
    wi_term = jnp.concatenate([pair_term, gate_term], axis=1)
    grad_normed = product_of("kerj,cke->rjc", grad_proj, w_pairs) + product_of(
        "rjd,cd->rjc", grad_gate, w_gate
    )
    grad_x = upstream + norm_grad(grad_normed, normed_full, inverse, -1)
    return (grad_x, wi_term)


def to_channels(stacked):
    return lax.all_to_all(stacked, ("chan", "sub"), split_axis=1, concat_axis=3, tiled=True)


def to_columns(stacked):
    return lax.all_to_all(stacked, ("chan", "sub"), split_axis=3, concat_axis=1, tiled=True)


def turn_rows(matrix):
    return lax.all_to_all(matrix, "row", split_axis=2, concat_axis=1, tiled=True)


def fold_rows(source, folder, initial):
    return folder(initial, lax.all_gather(source, "row", axis=1, tiled=True), jnp.int32(0))


def spread_part(pair, cotangent, token_mask, w_in, w_out):
    row_count, col_count, _ = pair.shape
    hidden = w_out.shape[1]
    token_total = token_mask.shape[0]
    row_id = lax.axis_index("row")
    col_id = lax.axis_index(("chan", "sub"))
    mask_full = token_mask.astype(jnp.float32)
    rows_mask = lax.dynamic_slice_in_dim(mask_full, row_id * row_count, row_count)
    cols_mask = lax.dynamic_slice_in_dim(mask_full, col_id * col_count, col_count)
    states = [pair]
    saved = []
    for layer_id in range(2):
        current = states[-1]
        pairs_local = front_block(current, rows_mask, cols_mask, w_in[layer_id], hidden)
        spread = to_channels(pairs_local)
        left_rows = spread[0]
        right_rows = spread[1]
        zero_tri = jnp.zeros(left_rows.shape, jnp.float32)
        keeper = None
        if layer_id == 0:

            def out_forward(totals, portion, offset):
                product_block = product_of("qrk,qjk->qrj", left_rows, portion)
                return product_block

            tri_rows = fold_rows(right_rows, out_forward, zero_tri)
        else:
            left_turned = turn_rows(left_rows)

            def in_forward(totals, portion, offset):
                return product_of("qki,qkj->qij", left_turned, portion)

            tri_rows = fold_rows(right_rows, in_forward, zero_tri)
        tri_cols = to_columns(tri_rows.astype(jnp.bfloat16)[None])[0]
        states.append(back_block(current, tri_cols, w_in[layer_id], w_out[layer_id], hidden))
        saved.append((left_rows, right_rows, tri_cols, keeper))
    upstream = cotangent.astype(jnp.float32)
    wi_grads = [None, None]
    wo_grads = [None, None]
    for layer_id in (1, 0):
        left_rows, right_rows, tri_cols, keeper = saved[layer_id]
        current = states[layer_id]
        grad_tri, wo_term = grad_back_block(
            current, tri_cols, upstream, w_in[layer_id], w_out[layer_id], hidden
        )
        grad_rows = to_channels(grad_tri[None])[0]
        zero_grad = jnp.zeros(left_rows.shape, jnp.float32)
        if layer_id == 1:

            def in_backward(carried, portion, offset):
                left_block = product_of("qkj,qij->qki", right_rows, portion)
                return (left_block, product_of("qki,qij->qkj", left_rows, portion))

            grad_left, grad_right = fold_rows(grad_rows, in_backward, (zero_grad, zero_grad))
        else:
            grad_turned = turn_rows(grad_rows)

            def right_step(totals, portion, offset):
                return product_of("qij,qik->qjk", grad_turned, portion)

            def left_step(totals, portion, offset):
                return product_of("qij,qjk->qik", grad_rows, portion)

            grad_left = fold_rows(right_rows, left_step, zero_grad)
            grad_right = fold_rows(left_rows, right_step, zero_grad)
        grad_pairs = to_columns(jnp.stack([grad_left, grad_right]).astype(jnp.bfloat16))
        upstream, wi_term = grad_front_block(
            current,
            tri_cols,
            grad_pairs,
            upstream,
            rows_mask,
            cols_mask,
            w_in[layer_id],
            w_out[layer_id],
            hidden,
        )
        wi_grads[layer_id] = wi_term
        wo_grads[layer_id] = wo_term
    wi_sum, wo_sum = lax.psum((jnp.stack(wi_grads), jnp.stack(wo_grads)), ("row", "chan", "sub"))
    return (states[2], upstream.astype(jnp.bfloat16), wi_sum / token_total, wo_sum / token_total)


def solution(mesh):
    sizes = tuple(mesh.shape[axis] for axis in ("row", "chan", "sub"))

    def shards(pair, cotangent, token_mask, w_in, w_out):
        tokens = token_mask.shape[0]
        tiled = tokens % (TILE * sizes[1] * sizes[2]) == 0
        if tiled and PLANES * tokens * tokens * pair.shape[-1] * 4 <= VMEM_PLAN:
            return whole_part(sizes, pair, cotangent, token_mask, w_in, w_out)
        return spread_part(pair, cotangent, token_mask, w_in, w_out)

    placed = (
        P(("groups", "row"), ("chan", "sub"), None),
        P(("groups", "row"), ("chan", "sub"), None),
        P("groups"),
        P(),
        P(),
    )
    return jax.shard_map(
        shards,
        mesh=mesh,
        in_specs=placed,
        out_specs=(
            P(("groups", "row"), ("chan", "sub"), None),
            P(("groups", "row"), ("chan", "sub"), None),
            P("groups", None, None),
            P("groups", None, None),
        ),
        check_vma=False,
    )
```

```python
import functools

import jax
import jax.numpy as jnp
from jax import lax
from jax.experimental import pallas as pl
from jax.experimental.pallas import tpu as pltpu
from jax.sharding import PartitionSpec as P

EPSILON = 1e-05
F32 = jnp.float32
BF16 = jnp.bfloat16
TILE = 8
PLANES = 40
FRONT = (1024, 1)
MIDDLE = (1024, 1)
TURN = (1024, 1)
DOWN = (1024, 1)
LAST = (1024, 1)
TRI_GROUP = 16
TRI_UNROLL = 2
VMEM_BYTES = 40 * 2**20
VMEM_PLAN = 40 * 2**20


def dot(left, right):
    return lax.dot_general(left, right, (((1,), (0,)), ((), ())), preferred_element_type=F32)


def dot_rows(left, right):
    return lax.dot_general(left, right, (((0,), (0,)), ((), ())), preferred_element_type=F32)


def dot_last(left, right):
    return lax.dot_general(left, right, (((1,), (1,)), ((), ())), preferred_element_type=F32)


def lane_mean(values):
    return jnp.mean(values, axis=-1, keepdims=True)


def norm_of(values):
    shifted = values - lane_mean(values)
    inverse = lax.rsqrt(lane_mean(shifted * shifted) + EPSILON)
    return shifted * inverse, inverse


def norm_back(upstream, normed, inverse):
    return inverse * (upstream - lane_mean(upstream) - normed * lane_mean(upstream * normed))


def rounded(values):
    return values.astype(BF16).astype(F32)


def unrounded(values):
    return values


KEEP_TRI = rounded
KEEP_STATE = rounded
KEEP_GRAD = rounded
KEEP_SIDE = rounded
KEEP_GTRI = rounded


def triangle(tokens, left, left_row, right, right_turned, target):
    tiles = tokens // TILE

    def right_tile(r, q):
        if right_turned:
            return right[pl.ds(q * TILE * tokens + r, TILE, stride=tokens), :]
        return right[pl.ds(r * tokens + q * TILE, TILE), :]

    def body(step, carry):
        first = step * TRI_GROUP
        totals = [[None] * tiles for _ in range(TRI_GROUP)]
        for r in range(tokens):
            column = [right_tile(r, q) for q in range(tiles)]
            for p in range(TRI_GROUP):
                scale = jnp.broadcast_to(left[pl.ds(left_row(first + p, r), 1), :], column[0].shape)
                for q in range(tiles):
                    term = scale * column[q]
                    totals[p][q] = term if r == 0 else totals[p][q] + term
        for p in range(TRI_GROUP):
            for q in range(tiles):
                at = pl.multiple_of((first + p) * tokens + q * TILE, TILE)
                target[pl.ds(at, TILE), :] = totals[p][q]
        return carry

    lax.fori_loop(0, tokens // TRI_GROUP, body, 0, unroll=TRI_UNROLL)


def whole_kernel(
    tokens, sizes, refs_in, mask_ref, w_in_ref, w_out_ref,
    updated_ref, pair_grad_ref, gwi_ref, gwo_ref,
    states, cot, flat, side, normed, inv, normed16, one_a, two_a, one_b, two_b,
    gate, tnorm, tinv, tnorm16, slope, tri, ga, gb,
    w_half, w_turned, wo_turned, gproj, gh, mask,
):
    n_row, n_chan, n_sub = sizes
    row_id, chan_id, sub_id = lax.axis_index("row"), lax.axis_index("chan"), lax.axis_index("sub")
    rows, cols = tokens // n_row, tokens // (n_chan * n_sub)
    pairs = tokens * tokens
    hidden = w_out_ref.shape[1]
    channels = w_in_ref.shape[1]
    gy_ref = cot

    place(tokens, sizes, refs_in, states.at[0], gy_ref)

    for u in range(2):
        w_turned[u] = w_in_ref[u].T
        wo_turned[u] = w_out_ref[u].T
        for k in range(5):
            at = slice(hidden * k, hidden * (k + 1))
            values = w_in_ref[u, :, at]
            w_half[u, :, at] = values * jnp.asarray(0.5, BF16) if k in (1, 3, 4) else values
    for j in range(tokens):
        mask[j : j + 1, :] = jnp.full((1, channels), mask_ref[j].astype(F32))

    def half_mask(step, chunk):
        lines = chunk // tokens
        outer = mask[pl.ds(step * lines, lines), :] * 0.5
        return (outer[:, None, :] * mask[...][None, :, :]).reshape(chunk, channels)

    def at_chunk(step, chunk):
        return pl.ds(pl.multiple_of(step * chunk, chunk), chunk)

    def front(u, x, step, chunk):
        here = at_chunk(step, chunk)
        n, s = norm_of(x)
        normed[u, here, :] = n
        inv[u, here, :] = jnp.broadcast_to(s, n.shape)
        n16 = n.astype(BF16)
        normed16[u, here, :] = n16
        projected = dot(n16, w_half[u])
        pa, qa, pb, qb, qz = [projected[:, hidden * k : hidden * (k + 1)] for k in range(5)]
        half = half_mask(step, chunk)
        for p, q, one, two, keep in ((pa, qa, one_a, two_a, flat), (pb, qb, one_b, two_b, side)):
            first = half * jnp.tanh(q) + half
            value = first * p
            one[u, here, :] = first
            two[u, here, :] = value - value * first
            keep[u, here, :] = KEEP_SIDE(value)
        gate[u, here, :] = 0.5 * jnp.tanh(qz) + 0.5

    def back(u, step, chunk):
        here = at_chunk(step, chunk)
        tn, r = norm_of(KEEP_TRI(tri[here, :]))
        tnorm[u, here, :] = tn
        tinv[u, here, :] = jnp.broadcast_to(r, tn.shape)
        tn16 = tn.astype(BF16)
        tnorm16[u, here, :] = tn16
        z = gate[u, here, :]
        gated = z * dot(tn16, w_out_ref[u])
        slope[u, here, :] = gated - gated * z
        return KEEP_STATE(states[u, here, :] + gated)

    def grad_back(u, gy, step, chunk):
        here = at_chunk(step, chunk)
        gh16 = (gy * gate[u, here, :]).astype(BF16)
        gh[here, :] = gh16
        gtri = norm_back(dot(gh16, wo_turned[u]), tnorm[u, here, :], tinv[u, here, :])
        tri[here, :] = KEEP_GTRI(gtri)

    def grad_front(u, gy, step, chunk):
        here = at_chunk(step, chunk)
        ga_here, gb_here = KEEP_GRAD(ga[here, :]), KEEP_GRAD(gb[here, :])
        pieces = [
            ga_here * one_a[u, here, :],
            ga_here * two_a[u, here, :],
            gb_here * one_b[u, here, :],
            gb_here * two_b[u, here, :],
            gy * slope[u, here, :],
        ]
        for k, piece in enumerate(pieces):
            gproj[here, hidden * k : hidden * (k + 1)] = piece.astype(BF16)

    def grad_state(u, gy, here):
        h = dot(gproj[here, :], w_turned[u])
        return gy + norm_back(h, normed[u, here, :], inv[u, here, :])

    def loop(body, chunk, unroll):
        def step_of(step, carry):
            body(step, chunk)
            return carry

        lax.fori_loop(0, pairs // chunk, step_of, 0, unroll=unroll)

    natural = lambda p, r: p * tokens + r
    turned = lambda p, r: r * tokens + p

    loop(lambda step, chunk: front(0, states[0, at_chunk(step, chunk), :], step, chunk), *FRONT)
    triangle(tokens, flat.at[0], natural, side.at[0], True, tri)

    def middle(step, chunk):
        x1 = back(0, step, chunk)
        states[1, at_chunk(step, chunk), :] = x1
        front(1, x1, step, chunk)

    loop(middle, *MIDDLE)
    triangle(tokens, flat.at[1], turned, side.at[1], False, tri)

    def turn(step, chunk):
        here = at_chunk(step, chunk)
        states[0, here, :] = back(1, step, chunk)
        grad_back(1, gy_ref[here, :], step, chunk)

    loop(turn, *TURN)
    gwo_ref[1] = dot_rows(tnorm16[1], gh[...]) * (1.0 / tokens)

    triangle(tokens, side.at[1], natural, tri, True, ga)
    triangle(tokens, flat.at[1], natural, tri, False, gb)

    def down(step, chunk):
        here = at_chunk(step, chunk)
        grad_front(1, gy_ref[here, :], step, chunk)
        gx = grad_state(1, gy_ref[here, :], here)
        gy_ref[here, :] = gx
        grad_back(0, gx, step, chunk)

    loop(down, *DOWN)
    gwi_ref[1] = dot_rows(normed16[1], gproj[...]) * (1.0 / tokens)
    gwo_ref[0] = dot_rows(tnorm16[0], gh[...]) * (1.0 / tokens)

    triangle(tokens, tri, natural, side.at[0], False, ga)
    triangle(tokens, tri, turned, flat.at[0], False, gb)

    def last(step, chunk):
        grad_front(0, gy_ref[at_chunk(step, chunk), :], step, chunk)

    loop(last, *LAST)
    own = rows * tokens
    here = pl.ds(pl.multiple_of(row_id * own, own), own)
    gy_ref[here, :] = grad_state(0, gy_ref[here, :], here)
    gwi_ref[0] = dot_rows(normed16[0], gproj[...]) * (1.0 / tokens)

    c0 = pl.multiple_of((chan_id * n_sub + sub_id) * cols, TILE)
    for source, target in ((states.at[0], updated_ref), (gy_ref, pair_grad_ref)):
        for r in range(rows):
            at = pl.multiple_of((row_id * rows + r) * tokens + c0, TILE)
            target[r] = source[pl.ds(at, cols), :].astype(BF16)


def place(tokens, sizes, refs_in, x_ref, gy_ref):
    n_row, n_chan, n_sub = sizes
    row_id, chan_id, sub_id = lax.axis_index("row"), lax.axis_index("chan"), lax.axis_index("sub")
    rows, cols = tokens // n_row, tokens // (n_chan * n_sub)
    channels = x_ref.shape[-1]
    for place_in_list, ref in enumerate(refs_in):
        chan_step, sub_step = place_in_list // n_sub, place_in_list % n_sub
        chan, sub = jnp.bitwise_xor(chan_id, chan_step), jnp.bitwise_xor(sub_id, sub_step)
        c0 = (chan * n_sub + sub) * cols
        for row_step in range(n_row):
            row = jnp.bitwise_xor(row_id, row_step)
            for kind, target in ((0, x_ref), (1, gy_ref)):
                block = ref[row_step, kind].astype(F32).reshape(rows, cols, channels)
                for r in range(rows):
                    at = pl.multiple_of((row * rows + r) * tokens + c0, TILE)
                    target[pl.ds(at, cols), :] = block[r]


def from_step(block, axis, size, step):
    return lax.ppermute(block, axis, [(i, i ^ step) for i in range(size)])


def gather_part(pair, cotangent, sizes):
    n_row, n_chan, n_sub = sizes
    channels = pair.shape[-1]
    mine = jnp.stack([pair.reshape(-1, channels), cotangent.reshape(-1, channels)])
    far = {step: from_step(mine, "row", n_row, step) for step in range(n_row - 1, 0, -1)}
    column = jnp.stack([mine] + [far[step] for step in range(1, n_row)])
    parts = []
    for chan_step in range(n_chan):
        near = column if chan_step == 0 else from_step(column, "chan", n_chan, chan_step)
        parts += [near if step == 0 else from_step(near, "sub", n_sub, step) for step in range(n_sub)]
    return parts


def whole_part(sizes, pair, cotangent, token_mask, w_in, w_out):
    tokens = token_mask.shape[0]
    channels = pair.shape[-1]
    hidden = w_out.shape[1]
    pairs = tokens * tokens
    parts = gather_part(pair, cotangent, sizes)
    plane = pltpu.VMEM((pairs, channels), F32)
    two = pltpu.VMEM((2, pairs, channels), F32)
    two16 = pltpu.VMEM((2, pairs, channels), BF16)
    vmem = pl.BlockSpec(memory_space=pltpu.VMEM)

    def kernel(*refs):
        count = len(parts)
        whole_kernel(tokens, sizes, refs[:count], *refs[count:])

    return pl.pallas_call(
        kernel,
        out_shape=(
            jax.ShapeDtypeStruct(pair.shape, BF16),
            jax.ShapeDtypeStruct(pair.shape, BF16),
            jax.ShapeDtypeStruct(w_in.shape, F32),
            jax.ShapeDtypeStruct(w_out.shape, F32),
        ),
        in_specs=[vmem] * len(parts) + [pl.BlockSpec(memory_space=pltpu.SMEM), vmem, vmem],
        out_specs=(vmem,) * 4,
        scratch_shapes=[
            two, plane, two, two, two, two, two16, two, two, two, two,
            two, two, two, two16, two, plane, plane, plane,
            pltpu.VMEM(w_in.shape, BF16),
            pltpu.VMEM((2, w_in.shape[2], channels), BF16),
            pltpu.VMEM((2, channels, hidden), BF16),
            pltpu.VMEM((pairs, w_in.shape[2]), BF16),
            pltpu.VMEM((pairs, channels), BF16),
            pltpu.VMEM((tokens, channels), F32),
        ],
        compiler_params=pltpu.CompilerParams(vmem_limit_bytes=VMEM_BYTES),
    )(*parts, token_mask, w_in, w_out)


def layer_norm(values, norm_axis):
    centre = jnp.mean(values, axis=norm_axis, keepdims=True)
    shifted = values - centre
    spread = jnp.mean(shifted * shifted, axis=norm_axis, keepdims=True)
    inverse = lax.rsqrt(spread + EPSILON)
    return (shifted * inverse, inverse)


def norm_grad(upstream, normed, inverse, norm_axis):
    return inverse * (
        upstream
        - jnp.mean(upstream, axis=norm_axis, keepdims=True)
        - normed * jnp.mean(upstream * normed, axis=norm_axis, keepdims=True)
    )


def product_of(pattern, left_op, right_op):
    return jnp.einsum(pattern, left_op, right_op, preferred_element_type=jnp.float32)


def split_weights(w_in_u, hidden):
    channels = w_in_u.shape[0]
    return (w_in_u[:, : 4 * hidden].reshape(channels, 4, hidden), w_in_u[:, 4 * hidden :])


def front_block(state_block, rows_mask, cols_mask, w_in_u, hidden):
    normed, _ = layer_norm(state_block.astype(jnp.float32), -1)
    normed = normed.astype(jnp.bfloat16)
    w_pairs, w_gate = split_weights(w_in_u, hidden)
    projected = product_of("rjc,cke->kerj", normed, w_pairs)
    pair_mask = rows_mask[:, None] * cols_mask[None, :]
    left_side = jax.nn.sigmoid(projected[1]) * projected[0] * pair_mask
    right_side = jax.nn.sigmoid(projected[3]) * projected[2] * pair_mask
    return jnp.stack([left_side, right_side]).astype(jnp.bfloat16)


def back_block(state_block, tri_block, w_in_u, w_out_u, hidden):
    normed, _ = layer_norm(state_block.astype(jnp.float32), -1)
    normed = normed.astype(jnp.bfloat16)
    _, w_gate = split_weights(w_in_u, hidden)
    gate_value = jax.nn.sigmoid(product_of("rjc,cd->rjd", normed, w_gate))
    tnorm, _ = layer_norm(tri_block.astype(jnp.float32), 0)
    linear = product_of("erj,ec->rjc", tnorm.astype(jnp.bfloat16), w_out_u)
    return (state_block.astype(jnp.float32) + gate_value * linear).astype(jnp.bfloat16)


def grad_back_block(state_block, tri_block, upstream, w_in_u, w_out_u, hidden):
    normed, _ = layer_norm(state_block.astype(jnp.float32), -1)
    normed = normed.astype(jnp.bfloat16)
    _, w_gate = split_weights(w_in_u, hidden)
    gate_value = jax.nn.sigmoid(product_of("rjc,cd->rjd", normed, w_gate))
    tnorm, inverse = layer_norm(tri_block.astype(jnp.float32), 0)
    tnorm_low = tnorm.astype(jnp.bfloat16)
    grad_hidden = (upstream * gate_value).astype(jnp.bfloat16)
    wo_term = product_of("erj,rjc->ec", tnorm_low, grad_hidden)
    grad_tn = product_of("rjc,ec->erj", grad_hidden, w_out_u)
    grad_tri = norm_grad(grad_tn, tnorm, inverse, 0).astype(jnp.bfloat16)
    return (grad_tri, wo_term)


def grad_front_block(
    state_block, tri_block, grad_pairs, upstream, rows_mask, cols_mask, w_in_u, w_out_u, hidden
):
    normed_full, inverse = layer_norm(state_block.astype(jnp.float32), -1)
    normed = normed_full.astype(jnp.bfloat16)
    w_pairs, w_gate = split_weights(w_in_u, hidden)
    projected = product_of("rjc,cke->kerj", normed, w_pairs)
    gate_value = jax.nn.sigmoid(product_of("rjc,cd->rjd", normed, w_gate))
    tnorm, _ = layer_norm(tri_block.astype(jnp.float32), 0)
    linear = product_of("erj,ec->rjc", tnorm.astype(jnp.bfloat16), w_out_u)
    grad_gate = (upstream * linear * gate_value * (1.0 - gate_value)).astype(jnp.bfloat16)
    pair_mask = rows_mask[:, None] * cols_mask[None, :]
    sig_left = jax.nn.sigmoid(projected[1])
    sig_right = jax.nn.sigmoid(projected[3])
    grad_left = grad_pairs[0].astype(jnp.float32) * pair_mask
    grad_right = grad_pairs[1].astype(jnp.float32) * pair_mask
    grad_proj = jnp.stack(
        [
            grad_left * sig_left,
            grad_left * projected[0] * sig_left * (1.0 - sig_left),
            grad_right * sig_right,
            grad_right * projected[2] * sig_right * (1.0 - sig_right),
        ]
    ).astype(jnp.bfloat16)
    channels = state_block.shape[2]
    pair_term = product_of("rjc,kerj->cke", normed, grad_proj).reshape(channels, 4 * hidden)
    gate_term = product_of("rjc,rjd->cd", normed, grad_gate)
    wi_term = jnp.concatenate([pair_term, gate_term], axis=1)
    grad_normed = product_of("kerj,cke->rjc", grad_proj, w_pairs) + product_of(
        "rjd,cd->rjc", grad_gate, w_gate
    )
    grad_x = upstream + norm_grad(grad_normed, normed_full, inverse, -1)
    return (grad_x, wi_term)


def to_channels(stacked):
    return lax.all_to_all(stacked, ("chan", "sub"), split_axis=1, concat_axis=3, tiled=True)


def to_columns(stacked):
    return lax.all_to_all(stacked, ("chan", "sub"), split_axis=3, concat_axis=1, tiled=True)


def turn_rows(matrix):
    return lax.all_to_all(matrix, "row", split_axis=2, concat_axis=1, tiled=True)


def fold_rows(source, folder, initial):
    return folder(initial, lax.all_gather(source, "row", axis=1, tiled=True), jnp.int32(0))


def spread_part(pair, cotangent, token_mask, w_in, w_out):
    row_count, col_count, _ = pair.shape
    hidden = w_out.shape[1]
    token_total = token_mask.shape[0]
    row_id = lax.axis_index("row")
    col_id = lax.axis_index(("chan", "sub"))
    mask_full = token_mask.astype(jnp.float32)
    rows_mask = lax.dynamic_slice_in_dim(mask_full, row_id * row_count, row_count)
    cols_mask = lax.dynamic_slice_in_dim(mask_full, col_id * col_count, col_count)
    states = [pair]
    saved = []
    for layer_id in range(2):
        current = states[-1]
        pairs_local = front_block(current, rows_mask, cols_mask, w_in[layer_id], hidden)
        spread = to_channels(pairs_local)
        left_rows = spread[0]
        right_rows = spread[1]
        zero_tri = jnp.zeros(left_rows.shape, jnp.float32)
        keeper = None
        if layer_id == 0:

            def out_forward(totals, portion, offset):
                product_block = product_of("qrk,qjk->qrj", left_rows, portion)
                return product_block

            tri_rows = fold_rows(right_rows, out_forward, zero_tri)
        else:
            left_turned = turn_rows(left_rows)

            def in_forward(totals, portion, offset):
                return product_of("qki,qkj->qij", left_turned, portion)

            tri_rows = fold_rows(right_rows, in_forward, zero_tri)
        tri_cols = to_columns(tri_rows.astype(jnp.bfloat16)[None])[0]
        states.append(back_block(current, tri_cols, w_in[layer_id], w_out[layer_id], hidden))
        saved.append((left_rows, right_rows, tri_cols, keeper))
    upstream = cotangent.astype(jnp.float32)
    wi_grads = [None, None]
    wo_grads = [None, None]
    for layer_id in (1, 0):
        left_rows, right_rows, tri_cols, keeper = saved[layer_id]
        current = states[layer_id]
        grad_tri, wo_term = grad_back_block(
            current, tri_cols, upstream, w_in[layer_id], w_out[layer_id], hidden
        )
        grad_rows = to_channels(grad_tri[None])[0]
        zero_grad = jnp.zeros(left_rows.shape, jnp.float32)
        if layer_id == 1:

            def in_backward(carried, portion, offset):
                left_block = product_of("qkj,qij->qki", right_rows, portion)
                return (left_block, product_of("qki,qij->qkj", left_rows, portion))

            grad_left, grad_right = fold_rows(grad_rows, in_backward, (zero_grad, zero_grad))
        else:
            grad_turned = turn_rows(grad_rows)

            def right_step(totals, portion, offset):
                return product_of("qij,qik->qjk", grad_turned, portion)

            def left_step(totals, portion, offset):
                return product_of("qij,qjk->qik", grad_rows, portion)

            grad_left = fold_rows(right_rows, left_step, zero_grad)
            grad_right = fold_rows(left_rows, right_step, zero_grad)
        grad_pairs = to_columns(jnp.stack([grad_left, grad_right]).astype(jnp.bfloat16))
        upstream, wi_term = grad_front_block(
            current,
            tri_cols,
            grad_pairs,
            upstream,
            rows_mask,
            cols_mask,
            w_in[layer_id],
            w_out[layer_id],
            hidden,
        )
        wi_grads[layer_id] = wi_term
        wo_grads[layer_id] = wo_term
    wi_sum, wo_sum = lax.psum((jnp.stack(wi_grads), jnp.stack(wo_grads)), ("row", "chan", "sub"))
    return (states[2], upstream.astype(jnp.bfloat16), wi_sum / token_total, wo_sum / token_total)


def solution(mesh):
    sizes = tuple(mesh.shape[axis] for axis in ("row", "chan", "sub"))

    def shards(pair, cotangent, token_mask, w_in, w_out):
        tokens = token_mask.shape[0]
        tiled = tokens % (TILE * sizes[1] * sizes[2]) == 0
        tiled = tiled and all(size & (size - 1) == 0 for size in sizes)
        if tiled and PLANES * tokens * tokens * pair.shape[-1] * 4 <= VMEM_PLAN:
            return whole_part(sizes, pair, cotangent, token_mask, w_in, w_out)
        return spread_part(pair, cotangent, token_mask, w_in, w_out)

    placed = (
        P(("groups", "row"), ("chan", "sub"), None),
        P(("groups", "row"), ("chan", "sub"), None),
        P("groups"),
        P(),
        P(),
    )
    return jax.shard_map(
        shards,
        mesh=mesh,
        in_specs=placed,
        out_specs=(
            P(("groups", "row"), ("chan", "sub"), None),
            P(("groups", "row"), ("chan", "sub"), None),
            P("groups", None, None),
            P("groups", None, None),
        ),
        check_vma=False,
    )
```

```python
import functools

import jax
import jax.numpy as jnp
from jax import lax
from jax.experimental import pallas as pl
from jax.experimental.pallas import tpu as pltpu
from jax.sharding import PartitionSpec as P

EPSILON = 1e-05
F32 = jnp.float32
BF16 = jnp.bfloat16
TILE = 8
X_PARTS = 2
PLANES = 40
FRONT = (1024, 1)
MIDDLE = (1024, 1)
TURN = (1024, 1)
DOWN = (1024, 1)
LAST = (1024, 1)
TRI_GROUP = 16
TRI_UNROLL = 2
VMEM_BYTES = 28 * 2**20
VMEM_PLAN = 40 * 2**20


def dot(left, right):
    return lax.dot_general(left, right, (((1,), (0,)), ((), ())), preferred_element_type=F32)


def dot_rows(left, right):
    return lax.dot_general(left, right, (((0,), (0,)), ((), ())), preferred_element_type=F32)


def dot_last(left, right):
    return lax.dot_general(left, right, (((1,), (1,)), ((), ())), preferred_element_type=F32)


def lane_mean(values):
    return jnp.mean(values, axis=-1, keepdims=True)


def norm_of(values):
    shifted = values - lane_mean(values)
    inverse = lax.rsqrt(lane_mean(shifted * shifted) + EPSILON)
    return shifted * inverse, inverse


def norm_back(upstream, normed, inverse):
    return inverse * (upstream - lane_mean(upstream) - normed * lane_mean(upstream * normed))


def rounded(values):
    return values.astype(BF16).astype(F32)


def unrounded(values):
    return values


KEEP_TRI = rounded
KEEP_STATE = rounded
KEEP_GRAD = rounded
KEEP_SIDE = rounded
KEEP_GTRI = rounded


def triangle(tokens, left, left_row, right, right_turned, target):
    tiles = tokens // TILE

    def right_tile(r, q):
        if right_turned:
            return right[pl.ds(q * TILE * tokens + r, TILE, stride=tokens), :]
        return right[pl.ds(r * tokens + q * TILE, TILE), :]

    def body(step, carry):
        first = step * TRI_GROUP
        totals = [[None] * tiles for _ in range(TRI_GROUP)]
        for r in range(tokens):
            column = [right_tile(r, q) for q in range(tiles)]
            for p in range(TRI_GROUP):
                scale = jnp.broadcast_to(left[pl.ds(left_row(first + p, r), 1), :], column[0].shape)
                for q in range(tiles):
                    term = scale * column[q]
                    totals[p][q] = term if r == 0 else totals[p][q] + term
        for p in range(TRI_GROUP):
            for q in range(tiles):
                at = pl.multiple_of((first + p) * tokens + q * TILE, TILE)
                target[pl.ds(at, TILE), :] = totals[p][q]
        return carry

    lax.fori_loop(0, tokens // TRI_GROUP, body, 0, unroll=TRI_UNROLL)


def whole_kernel(
    tokens, sizes, pieces, refs_in, mask_hbm, w_in_hbm, w_out_hbm,
    updated_ref, pair_grad_ref, gwi_ref, gwo_ref,
    states, cot, flat, side, normed, inv, normed16, one_a, two_a, one_b, two_b,
    gate, tnorm, tinv, tnorm16, slope, tri, ga, gb,
    w_half, w_turned, wo_turned, gproj, gh, mask, mask_ref, w_in_ref, w_out_ref, sem,
):
    n_row, n_chan, n_sub = sizes
    row_id, chan_id, sub_id = lax.axis_index("row"), lax.axis_index("chan"), lax.axis_index("sub")
    rows, cols = tokens // n_row, tokens // (n_chan * n_sub)
    pairs = tokens * tokens
    hidden = w_out_ref.shape[1]
    channels = w_in_ref.shape[1]
    gy_ref = cot

    copies = [
        pltpu.make_async_copy(source, target, sem.at[k])
        for k, (source, target) in enumerate(((mask_hbm, mask_ref), (w_in_hbm, w_in_ref), (w_out_hbm, w_out_ref)))
    ]
    for copy in copies:
        copy.start()
    place(tokens, sizes, pieces, refs_in, states.at[0], gy_ref)
    for copy in copies:
        copy.wait()

    for u in range(2):
        w_turned[u] = w_in_ref[u].T
        wo_turned[u] = w_out_ref[u].T
        for k in range(5):
            at = slice(hidden * k, hidden * (k + 1))
            values = w_in_ref[u, :, at]
            w_half[u, :, at] = values * jnp.asarray(0.5, BF16) if k in (1, 3, 4) else values
    for j in range(tokens):
        mask[j : j + 1, :] = jnp.full((1, channels), mask_ref[j].astype(F32))

    def half_mask(step, chunk):
        lines = chunk // tokens
        outer = mask[pl.ds(step * lines, lines), :] * 0.5
        return (outer[:, None, :] * mask[...][None, :, :]).reshape(chunk, channels)

    def at_chunk(step, chunk):
        return pl.ds(pl.multiple_of(step * chunk, chunk), chunk)

    def front(u, x, step, chunk):
        here = at_chunk(step, chunk)
        n, s = norm_of(x)
        normed[u, here, :] = n
        inv[u, here, :] = jnp.broadcast_to(s, n.shape)
        n16 = n.astype(BF16)
        normed16[u, here, :] = n16
        projected = dot(n16, w_half[u])
        pa, qa, pb, qb, qz = [projected[:, hidden * k : hidden * (k + 1)] for k in range(5)]
        half = half_mask(step, chunk)
        for p, q, one, two, keep in ((pa, qa, one_a, two_a, flat), (pb, qb, one_b, two_b, side)):
            first = half * jnp.tanh(q) + half
            value = first * p
            one[u, here, :] = first
            two[u, here, :] = value - value * first
            keep[u, here, :] = KEEP_SIDE(value)
        gate[u, here, :] = 0.5 * jnp.tanh(qz) + 0.5

    def back(u, step, chunk):
        here = at_chunk(step, chunk)
        tn, r = norm_of(KEEP_TRI(tri[here, :]))
        tnorm[u, here, :] = tn
        tinv[u, here, :] = jnp.broadcast_to(r, tn.shape)
        tn16 = tn.astype(BF16)
        tnorm16[u, here, :] = tn16
        z = gate[u, here, :]
        gated = z * dot(tn16, w_out_ref[u])
        slope[u, here, :] = gated - gated * z
        return KEEP_STATE(states[u, here, :] + gated)

    def grad_back(u, gy, step, chunk):
        here = at_chunk(step, chunk)
        gh16 = (gy * gate[u, here, :]).astype(BF16)
        gh[here, :] = gh16
        gtri = norm_back(dot(gh16, wo_turned[u]), tnorm[u, here, :], tinv[u, here, :])
        tri[here, :] = KEEP_GTRI(gtri)

    def grad_front(u, gy, step, chunk):
        here = at_chunk(step, chunk)
        ga_here, gb_here = KEEP_GRAD(ga[here, :]), KEEP_GRAD(gb[here, :])
        pieces = [
            ga_here * one_a[u, here, :],
            ga_here * two_a[u, here, :],
            gb_here * one_b[u, here, :],
            gb_here * two_b[u, here, :],
            gy * slope[u, here, :],
        ]
        for k, piece in enumerate(pieces):
            gproj[here, hidden * k : hidden * (k + 1)] = piece.astype(BF16)

    def grad_state(u, gy, here):
        h = dot(gproj[here, :], w_turned[u])
        return gy + norm_back(h, normed[u, here, :], inv[u, here, :])

    def loop(body, chunk, unroll):
        def step_of(step, carry):
            body(step, chunk)
            return carry

        lax.fori_loop(0, pairs // chunk, step_of, 0, unroll=unroll)

    natural = lambda p, r: p * tokens + r
    turned = lambda p, r: r * tokens + p

    loop(lambda step, chunk: front(0, states[0, at_chunk(step, chunk), :], step, chunk), *FRONT)
    triangle(tokens, flat.at[0], natural, side.at[0], True, tri)

    def middle(step, chunk):
        x1 = back(0, step, chunk)
        states[1, at_chunk(step, chunk), :] = x1
        front(1, x1, step, chunk)

    loop(middle, *MIDDLE)
    triangle(tokens, flat.at[1], turned, side.at[1], False, tri)

    def turn(step, chunk):
        here = at_chunk(step, chunk)
        states[0, here, :] = back(1, step, chunk)
        grad_back(1, gy_ref[here, :], step, chunk)

    loop(turn, *TURN)
    gwo_ref[1] = dot_rows(tnorm16[1], gh[...]) * (1.0 / tokens)

    triangle(tokens, side.at[1], natural, tri, True, ga)
    triangle(tokens, flat.at[1], natural, tri, False, gb)

    def down(step, chunk):
        here = at_chunk(step, chunk)
        grad_front(1, gy_ref[here, :], step, chunk)
        gx = grad_state(1, gy_ref[here, :], here)
        gy_ref[here, :] = gx
        grad_back(0, gx, step, chunk)

    loop(down, *DOWN)
    gwi_ref[1] = dot_rows(normed16[1], gproj[...]) * (1.0 / tokens)
    gwo_ref[0] = dot_rows(tnorm16[0], gh[...]) * (1.0 / tokens)

    triangle(tokens, tri, natural, side.at[0], False, ga)
    triangle(tokens, tri, turned, flat.at[0], False, gb)

    def last(step, chunk):
        grad_front(0, gy_ref[at_chunk(step, chunk), :], step, chunk)

    loop(last, *LAST)
    own = rows * tokens
    here = pl.ds(pl.multiple_of(row_id * own, own), own)
    gy_ref[here, :] = grad_state(0, gy_ref[here, :], here)
    gwi_ref[0] = dot_rows(normed16[0], gproj[...]) * (1.0 / tokens)

    c0 = pl.multiple_of((chan_id * n_sub + sub_id) * cols, TILE)
    for source, target in ((states.at[0], updated_ref), (gy_ref, pair_grad_ref)):
        for r in range(rows):
            at = pl.multiple_of((row_id * rows + r) * tokens + c0, TILE)
            target[r] = source[pl.ds(at, cols), :].astype(BF16)


def place(tokens, sizes, pieces, refs_in, x_ref, gy_ref):
    n_row, n_chan, n_sub = sizes
    row_id, chan_id, sub_id = lax.axis_index("row"), lax.axis_index("chan"), lax.axis_index("sub")
    rows, cols = tokens // n_row, tokens // (n_chan * n_sub)
    channels = x_ref.shape[-1]
    for ref, (row_steps, chan_step, sub_step) in zip(refs_in, pieces):
        chan, sub = jnp.bitwise_xor(chan_id, chan_step), jnp.bitwise_xor(sub_id, sub_step)
        c0 = (chan * n_sub + sub) * cols
        for k, row_step in enumerate(row_steps):
            row = jnp.bitwise_xor(row_id, row_step)
            for kind, target in ((0, x_ref), (1, gy_ref)):
                block = ref[k, kind].astype(F32).reshape(rows, cols, channels)
                for r in range(rows):
                    at = pl.multiple_of((row * rows + r) * tokens + c0, TILE)
                    target[pl.ds(at, cols), :] = block[r]


def from_step(block, axis, size, step):
    return lax.ppermute(block, axis, [(i, i ^ step) for i in range(size)])


def gather_part(pair, cotangent, sizes):
    n_row, n_chan, n_sub = sizes
    channels = pair.shape[-1]
    mine = jnp.stack([pair.reshape(-1, channels), cotangent.reshape(-1, channels)])
    row_steps = [0] + list(range(n_row - 1, 0, -1))
    column = jnp.stack([mine] + [from_step(mine, "row", n_row, step) for step in row_steps[1:]])
    parts = [column]
    pieces = [(row_steps, 0, 0)]
    cut = max(n_row // X_PARTS, 1)
    for chan_step in range(1, n_chan):
        for first in range(0, n_row, cut):
            parts.append(from_step(column[first : first + cut], "chan", n_chan, chan_step))
            pieces.append((row_steps[first : first + cut], chan_step, 0))
    for part, (steps, chan_step, _) in list(zip(parts, pieces)):
        for sub_step in range(1, n_sub):
            parts.append(from_step(part, "sub", n_sub, sub_step))
            pieces.append((steps, chan_step, sub_step))
    return parts, pieces


def whole_part(sizes, pair, cotangent, token_mask, w_in, w_out):
    tokens = token_mask.shape[0]
    channels = pair.shape[-1]
    hidden = w_out.shape[1]
    pairs = tokens * tokens
    parts, pieces = gather_part(pair, cotangent, sizes)
    plane = pltpu.VMEM((pairs, channels), F32)
    two = pltpu.VMEM((2, pairs, channels), F32)
    two16 = pltpu.VMEM((2, pairs, channels), BF16)
    vmem = pl.BlockSpec(memory_space=pltpu.VMEM)

    def kernel(*refs):
        count = len(parts)
        whole_kernel(tokens, sizes, pieces, refs[:count], *refs[count:])

    return pl.pallas_call(
        kernel,
        out_shape=(
            jax.ShapeDtypeStruct(pair.shape, BF16),
            jax.ShapeDtypeStruct(pair.shape, BF16),
            jax.ShapeDtypeStruct(w_in.shape, F32),
            jax.ShapeDtypeStruct(w_out.shape, F32),
        ),
        in_specs=[vmem] * len(parts) + [pl.BlockSpec(memory_space=pltpu.HBM)] * 3,
        out_specs=(vmem,) * 4,
        scratch_shapes=[
            two, plane, two, two, two, two, two16, two, two, two, two,
            two, two, two, two16, two, plane, plane, plane,
            pltpu.VMEM(w_in.shape, BF16),
            pltpu.VMEM((2, w_in.shape[2], channels), BF16),
            pltpu.VMEM((2, channels, hidden), BF16),
            pltpu.VMEM((pairs, w_in.shape[2]), BF16),
            pltpu.VMEM((pairs, channels), BF16),
            pltpu.VMEM((tokens, channels), F32),
            pltpu.SMEM((tokens,), jnp.int32),
            pltpu.VMEM(w_in.shape, BF16),
            pltpu.VMEM(w_out.shape, BF16),
            pltpu.SemaphoreType.DMA((3,)),
        ],
        compiler_params=pltpu.CompilerParams(vmem_limit_bytes=VMEM_BYTES),
    )(*parts, token_mask, w_in, w_out)


def layer_norm(values, norm_axis):
    centre = jnp.mean(values, axis=norm_axis, keepdims=True)
    shifted = values - centre
    spread = jnp.mean(shifted * shifted, axis=norm_axis, keepdims=True)
    inverse = lax.rsqrt(spread + EPSILON)
    return (shifted * inverse, inverse)


def norm_grad(upstream, normed, inverse, norm_axis):
    return inverse * (
        upstream
        - jnp.mean(upstream, axis=norm_axis, keepdims=True)
        - normed * jnp.mean(upstream * normed, axis=norm_axis, keepdims=True)
    )


def product_of(pattern, left_op, right_op):
    return jnp.einsum(pattern, left_op, right_op, preferred_element_type=jnp.float32)


def split_weights(w_in_u, hidden):
    channels = w_in_u.shape[0]
    return (w_in_u[:, : 4 * hidden].reshape(channels, 4, hidden), w_in_u[:, 4 * hidden :])


def front_block(state_block, rows_mask, cols_mask, w_in_u, hidden):
    normed, _ = layer_norm(state_block.astype(jnp.float32), -1)
    normed = normed.astype(jnp.bfloat16)
    w_pairs, w_gate = split_weights(w_in_u, hidden)
    projected = product_of("rjc,cke->kerj", normed, w_pairs)
    pair_mask = rows_mask[:, None] * cols_mask[None, :]
    left_side = jax.nn.sigmoid(projected[1]) * projected[0] * pair_mask
    right_side = jax.nn.sigmoid(projected[3]) * projected[2] * pair_mask
    return jnp.stack([left_side, right_side]).astype(jnp.bfloat16)


def back_block(state_block, tri_block, w_in_u, w_out_u, hidden):
    normed, _ = layer_norm(state_block.astype(jnp.float32), -1)
    normed = normed.astype(jnp.bfloat16)
    _, w_gate = split_weights(w_in_u, hidden)
    gate_value = jax.nn.sigmoid(product_of("rjc,cd->rjd", normed, w_gate))
    tnorm, _ = layer_norm(tri_block.astype(jnp.float32), 0)
    linear = product_of("erj,ec->rjc", tnorm.astype(jnp.bfloat16), w_out_u)
    return (state_block.astype(jnp.float32) + gate_value * linear).astype(jnp.bfloat16)


def grad_back_block(state_block, tri_block, upstream, w_in_u, w_out_u, hidden):
    normed, _ = layer_norm(state_block.astype(jnp.float32), -1)
    normed = normed.astype(jnp.bfloat16)
    _, w_gate = split_weights(w_in_u, hidden)
    gate_value = jax.nn.sigmoid(product_of("rjc,cd->rjd", normed, w_gate))
    tnorm, inverse = layer_norm(tri_block.astype(jnp.float32), 0)
    tnorm_low = tnorm.astype(jnp.bfloat16)
    grad_hidden = (upstream * gate_value).astype(jnp.bfloat16)
    wo_term = product_of("erj,rjc->ec", tnorm_low, grad_hidden)
    grad_tn = product_of("rjc,ec->erj", grad_hidden, w_out_u)
    grad_tri = norm_grad(grad_tn, tnorm, inverse, 0).astype(jnp.bfloat16)
    return (grad_tri, wo_term)


def grad_front_block(
    state_block, tri_block, grad_pairs, upstream, rows_mask, cols_mask, w_in_u, w_out_u, hidden
):
    normed_full, inverse = layer_norm(state_block.astype(jnp.float32), -1)
    normed = normed_full.astype(jnp.bfloat16)
    w_pairs, w_gate = split_weights(w_in_u, hidden)
    projected = product_of("rjc,cke->kerj", normed, w_pairs)
    gate_value = jax.nn.sigmoid(product_of("rjc,cd->rjd", normed, w_gate))
    tnorm, _ = layer_norm(tri_block.astype(jnp.float32), 0)
    linear = product_of("erj,ec->rjc", tnorm.astype(jnp.bfloat16), w_out_u)
    grad_gate = (upstream * linear * gate_value * (1.0 - gate_value)).astype(jnp.bfloat16)
    pair_mask = rows_mask[:, None] * cols_mask[None, :]
    sig_left = jax.nn.sigmoid(projected[1])
    sig_right = jax.nn.sigmoid(projected[3])
    grad_left = grad_pairs[0].astype(jnp.float32) * pair_mask
    grad_right = grad_pairs[1].astype(jnp.float32) * pair_mask
    grad_proj = jnp.stack(
        [
            grad_left * sig_left,
            grad_left * projected[0] * sig_left * (1.0 - sig_left),
            grad_right * sig_right,
            grad_right * projected[2] * sig_right * (1.0 - sig_right),
        ]
    ).astype(jnp.bfloat16)
    channels = state_block.shape[2]
    pair_term = product_of("rjc,kerj->cke", normed, grad_proj).reshape(channels, 4 * hidden)
    gate_term = product_of("rjc,rjd->cd", normed, grad_gate)
    wi_term = jnp.concatenate([pair_term, gate_term], axis=1)
    grad_normed = product_of("kerj,cke->rjc", grad_proj, w_pairs) + product_of(
        "rjd,cd->rjc", grad_gate, w_gate
    )
    grad_x = upstream + norm_grad(grad_normed, normed_full, inverse, -1)
    return (grad_x, wi_term)


def to_channels(stacked):
    return lax.all_to_all(stacked, ("chan", "sub"), split_axis=1, concat_axis=3, tiled=True)


def to_columns(stacked):
    return lax.all_to_all(stacked, ("chan", "sub"), split_axis=3, concat_axis=1, tiled=True)


def turn_rows(matrix):
    return lax.all_to_all(matrix, "row", split_axis=2, concat_axis=1, tiled=True)


def fold_rows(source, folder, initial):
    return folder(initial, lax.all_gather(source, "row", axis=1, tiled=True), jnp.int32(0))


def spread_part(pair, cotangent, token_mask, w_in, w_out):
    row_count, col_count, _ = pair.shape
    hidden = w_out.shape[1]
    token_total = token_mask.shape[0]
    row_id = lax.axis_index("row")
    col_id = lax.axis_index(("chan", "sub"))
    mask_full = token_mask.astype(jnp.float32)
    rows_mask = lax.dynamic_slice_in_dim(mask_full, row_id * row_count, row_count)
    cols_mask = lax.dynamic_slice_in_dim(mask_full, col_id * col_count, col_count)
    states = [pair]
    saved = []
    for layer_id in range(2):
        current = states[-1]
        pairs_local = front_block(current, rows_mask, cols_mask, w_in[layer_id], hidden)
        spread = to_channels(pairs_local)
        left_rows = spread[0]
        right_rows = spread[1]
        zero_tri = jnp.zeros(left_rows.shape, jnp.float32)
        keeper = None
        if layer_id == 0:

            def out_forward(totals, portion, offset):
                product_block = product_of("qrk,qjk->qrj", left_rows, portion)
                return product_block

            tri_rows = fold_rows(right_rows, out_forward, zero_tri)
        else:
            left_turned = turn_rows(left_rows)

            def in_forward(totals, portion, offset):
                return product_of("qki,qkj->qij", left_turned, portion)

            tri_rows = fold_rows(right_rows, in_forward, zero_tri)
        tri_cols = to_columns(tri_rows.astype(jnp.bfloat16)[None])[0]
        states.append(back_block(current, tri_cols, w_in[layer_id], w_out[layer_id], hidden))
        saved.append((left_rows, right_rows, tri_cols, keeper))
    upstream = cotangent.astype(jnp.float32)
    wi_grads = [None, None]
    wo_grads = [None, None]
    for layer_id in (1, 0):
        left_rows, right_rows, tri_cols, keeper = saved[layer_id]
        current = states[layer_id]
        grad_tri, wo_term = grad_back_block(
            current, tri_cols, upstream, w_in[layer_id], w_out[layer_id], hidden
        )
        grad_rows = to_channels(grad_tri[None])[0]
        zero_grad = jnp.zeros(left_rows.shape, jnp.float32)
        if layer_id == 1:

            def in_backward(carried, portion, offset):
                left_block = product_of("qkj,qij->qki", right_rows, portion)
                return (left_block, product_of("qki,qij->qkj", left_rows, portion))

            grad_left, grad_right = fold_rows(grad_rows, in_backward, (zero_grad, zero_grad))
        else:
            grad_turned = turn_rows(grad_rows)

            def right_step(totals, portion, offset):
                return product_of("qij,qik->qjk", grad_turned, portion)

            def left_step(totals, portion, offset):
                return product_of("qij,qjk->qik", grad_rows, portion)

            grad_left = fold_rows(right_rows, left_step, zero_grad)
            grad_right = fold_rows(left_rows, right_step, zero_grad)
        grad_pairs = to_columns(jnp.stack([grad_left, grad_right]).astype(jnp.bfloat16))
        upstream, wi_term = grad_front_block(
            current,
            tri_cols,
            grad_pairs,
            upstream,
            rows_mask,
            cols_mask,
            w_in[layer_id],
            w_out[layer_id],
            hidden,
        )
        wi_grads[layer_id] = wi_term
        wo_grads[layer_id] = wo_term
    wi_sum, wo_sum = lax.psum((jnp.stack(wi_grads), jnp.stack(wo_grads)), ("row", "chan", "sub"))
    return (states[2], upstream.astype(jnp.bfloat16), wi_sum / token_total, wo_sum / token_total)


def solution(mesh):
    sizes = tuple(mesh.shape[axis] for axis in ("row", "chan", "sub"))

    def shards(pair, cotangent, token_mask, w_in, w_out):
        tokens = token_mask.shape[0]
        tiled = tokens % (TILE * sizes[1] * sizes[2]) == 0
        tiled = tiled and all(size & (size - 1) == 0 for size in sizes)
        if tiled and PLANES * tokens * tokens * pair.shape[-1] * 4 <= VMEM_PLAN:
            return whole_part(sizes, pair, cotangent, token_mask, w_in, w_out)
        return spread_part(pair, cotangent, token_mask, w_in, w_out)

    placed = (
        P(("groups", "row"), ("chan", "sub"), None),
        P(("groups", "row"), ("chan", "sub"), None),
        P("groups"),
        P(),
        P(),
    )
    return jax.shard_map(
        shards,
        mesh=mesh,
        in_specs=placed,
        out_specs=(
            P(("groups", "row"), ("chan", "sub"), None),
            P(("groups", "row"), ("chan", "sub"), None),
            P("groups", None, None),
            P("groups", None, None),
        ),
        check_vma=False,
    )
```

```python
import functools

import jax
import jax.numpy as jnp
from jax import lax
from jax.experimental import pallas as pl
from jax.experimental.pallas import tpu as pltpu
from jax.sharding import PartitionSpec as P

EPSILON = 1e-05
F32 = jnp.float32
BF16 = jnp.bfloat16
TILE = 8
X_PARTS = 2
TILE16 = 16
SUM = 8
PLANES = 40
FRONT = (1024, 1)
MIDDLE = (1024, 1)
TURN = (1024, 1)
DOWN = (1024, 1)
LAST = (1024, 1)
TRI_GROUP = 8
TRI_UNROLL = 4
VMEM_BYTES = 28 * 2**20
VMEM_PLAN = 40 * 2**20


def dot(left, right):
    return lax.dot_general(left, right, (((1,), (0,)), ((), ())), preferred_element_type=F32)


def dot_rows(left, right):
    return lax.dot_general(left, right, (((0,), (0,)), ((), ())), preferred_element_type=F32)


def dot_last(left, right):
    return lax.dot_general(left, right, (((1,), (1,)), ((), ())), preferred_element_type=F32)


def lane_mean(values):
    return jnp.mean(values, axis=-1, keepdims=True)


def norm_of(values16):
    channels = values16.shape[-1]
    shifted = values16.astype(F32) - dot(values16, jnp.full((channels, channels), 1.0 / channels, BF16))
    inverse = lax.rsqrt(lane_mean(shifted * shifted) + EPSILON)
    return shifted * inverse, inverse


def norm_back(upstream, normed, inverse):
    return inverse * (upstream - lane_mean(upstream) - normed * lane_mean(upstream * normed))


def rounded(values):
    return values.astype(BF16).astype(F32)


def unrounded(values):
    return values


KEEP_TRI = rounded
KEEP_STATE = rounded
KEEP_GRAD = rounded


def triangle(tokens, left, left_row, right16, target):
    channels = target.shape[-1]
    tiles = tokens // TILE16

    def body(step, carry):
        first = step * TRI_GROUP
        totals = [[None] * tiles for _ in range(TRI_GROUP)]
        for g in range(0, tokens, SUM):
            terms = [[[] for _ in range(tiles)] for _ in range(TRI_GROUP)]
            for r in range(g, g + SUM):
                column = [right16[pl.ds(r * tokens + q * TILE16, TILE16), :] for q in range(tiles)]
                for p in range(TRI_GROUP):
                    scale = left[pl.ds(left_row(first + p, r), 1), :]
                    scale = jnp.broadcast_to(scale, (TILE16, channels)).astype(BF16)
                    for q in range(tiles):
                        level = terms[p][q]
                        level.append((scale * column[q], 1))
                        while len(level) > 1 and level[-1][1] == level[-2][1]:
                            (last, size), (other, _) = level.pop(), level.pop()
                            level.append((other + last, 2 * size))
            for p in range(TRI_GROUP):
                for q in range(tiles):
                    value = terms[p][q][0][0].astype(F32)
                    totals[p][q] = value if g == 0 else totals[p][q] + value
        for p in range(TRI_GROUP):
            for q in range(tiles):
                at = pl.multiple_of((first + p) * tokens + q * TILE16, TILE16)
                target[pl.ds(at, TILE16), :] = totals[p][q]
        return carry

    lax.fori_loop(0, tokens // TRI_GROUP, body, 0, unroll=TRI_UNROLL)


def whole_kernel(
    tokens, sizes, pieces, refs_in, mask_hbm, w_in_hbm, w_out_hbm,
    updated_ref, pair_grad_ref, gwi_ref, gwo_ref,
    states, cot, flat, side, flat16, side16, normed, inv, normed16, one_a, two_a, one_b, two_b,
    gate, tnorm, tinv, tnorm16, slope, tri, tri16, turned16, ga, gb,
    w_half, w_turned, wo_turned, gproj, gh, mask, mask_ref, w_in_ref, w_out_ref, sem,
):
    n_row, n_chan, n_sub = sizes
    row_id, chan_id, sub_id = lax.axis_index("row"), lax.axis_index("chan"), lax.axis_index("sub")
    rows, cols = tokens // n_row, tokens // (n_chan * n_sub)
    pairs = tokens * tokens
    hidden = w_out_ref.shape[1]
    channels = w_in_ref.shape[1]
    gy_ref = cot

    copies = [
        pltpu.make_async_copy(source, target, sem.at[k])
        for k, (source, target) in enumerate(((mask_hbm, mask_ref), (w_in_hbm, w_in_ref), (w_out_hbm, w_out_ref)))
    ]
    for copy in copies:
        copy.start()
    place(tokens, sizes, pieces, refs_in, states.at[0], gy_ref)
    for copy in copies:
        copy.wait()

    for u in range(2):
        w_turned[u] = w_in_ref[u].T
        wo_turned[u] = w_out_ref[u].T
        for k in range(5):
            at = slice(hidden * k, hidden * (k + 1))
            values = w_in_ref[u, :, at]
            w_half[u, :, at] = values * jnp.asarray(0.5, BF16) if k in (1, 3, 4) else values
    for j in range(tokens):
        mask[j : j + 1, :] = jnp.full((1, channels), mask_ref[j].astype(F32))

    def half_mask(step, chunk):
        lines = chunk // tokens
        outer = mask[pl.ds(step * lines, lines), :] * 0.5
        return (outer[:, None, :] * mask[...][None, :, :]).reshape(chunk, channels)

    def at_chunk(step, chunk):
        return pl.ds(pl.multiple_of(step * chunk, chunk), chunk)

    def front(u, x16, step, chunk):
        here = at_chunk(step, chunk)
        n, s = norm_of(x16)
        normed[u, here, :] = n
        inv[u, here, :] = jnp.broadcast_to(s, n.shape)
        n16 = n.astype(BF16)
        normed16[u, here, :] = n16
        projected = dot(n16, w_half[u])
        pa, qa, pb, qb, qz = [projected[:, hidden * k : hidden * (k + 1)] for k in range(5)]
        half = half_mask(step, chunk)
        for p, q, one, two, keep, keep16 in (
            (pa, qa, one_a, two_a, flat, flat16),
            (pb, qb, one_b, two_b, side, side16),
        ):
            first = half * jnp.tanh(q) + half
            value = first * p
            one[u, here, :] = first
            two[u, here, :] = value - value * first
            keep[u, here, :] = value
            keep16[u, here, :] = value.astype(BF16)
        gate[u, here, :] = 0.5 * jnp.tanh(qz) + 0.5

    def back(u, step, chunk):
        here = at_chunk(step, chunk)
        tn, r = norm_of(tri[here, :].astype(BF16))
        tnorm[u, here, :] = tn
        tinv[u, here, :] = jnp.broadcast_to(r, tn.shape)
        tn16 = tn.astype(BF16)
        tnorm16[u, here, :] = tn16
        z = gate[u, here, :]
        gated = z * dot(tn16, w_out_ref[u])
        slope[u, here, :] = gated - gated * z
        return (states[u, here, :] + gated).astype(BF16)

    def grad_back(u, gy, step, chunk):
        here = at_chunk(step, chunk)
        gh16 = (gy * gate[u, here, :]).astype(BF16)
        gh[here, :] = gh16
        gtri = norm_back(dot(gh16, wo_turned[u]), tnorm[u, here, :], tinv[u, here, :])
        tri[here, :] = gtri
        if u == 1:
            tri16[here, :] = gtri.astype(BF16)

    def grad_front(u, gy, step, chunk):
        here = at_chunk(step, chunk)
        ga_here, gb_here = KEEP_GRAD(ga[here, :]), KEEP_GRAD(gb[here, :])
        pieces = [
            ga_here * one_a[u, here, :],
            ga_here * two_a[u, here, :],
            gb_here * one_b[u, here, :],
            gb_here * two_b[u, here, :],
            gy * slope[u, here, :],
        ]
        for k, piece in enumerate(pieces):
            gproj[here, hidden * k : hidden * (k + 1)] = piece.astype(BF16)

    def grad_state(u, gy, here):
        h = dot(gproj[here, :], w_turned[u])
        return gy + norm_back(h, normed[u, here, :], inv[u, here, :])

    def loop(body, chunk, unroll):
        def step_of(step, carry):
            body(step, chunk)
            return carry

        lax.fori_loop(0, pairs // chunk, step_of, 0, unroll=unroll)

    def turn_pairs(source):
        for r in range(tokens):
            for q in range(tokens // TILE16):
                halves = [
                    source[pl.ds((q * TILE16 + half) * tokens + r, TILE, stride=tokens), :] for half in (0, TILE)
                ]
                at = r * tokens + q * TILE16
                turned16[at : at + TILE16, :] = jnp.concatenate(halves, axis=0).astype(BF16)

    natural = lambda p, r: p * tokens + r
    turned = lambda p, r: r * tokens + p

    loop(lambda step, chunk: front(0, states[0, at_chunk(step, chunk), :].astype(BF16), step, chunk), *FRONT)
    turn_pairs(side.at[0])
    triangle(tokens, flat.at[0], natural, turned16, tri)

    def middle(step, chunk):
        x1 = back(0, step, chunk)
        states[1, at_chunk(step, chunk), :] = x1.astype(F32)
        front(1, x1, step, chunk)

    loop(middle, *MIDDLE)
    triangle(tokens, flat.at[1], turned, side16.at[1], tri)

    def turn(step, chunk):
        here = at_chunk(step, chunk)
        states[0, here, :] = back(1, step, chunk).astype(F32)
        grad_back(1, gy_ref[here, :], step, chunk)

    loop(turn, *TURN)
    gwo_ref[1] = dot_rows(tnorm16[1], gh[...]) * (1.0 / tokens)

    turn_pairs(tri)
    triangle(tokens, side.at[1], natural, turned16, ga)
    triangle(tokens, flat.at[1], natural, tri16, gb)

    def down(step, chunk):
        here = at_chunk(step, chunk)
        grad_front(1, gy_ref[here, :], step, chunk)
        gx = grad_state(1, gy_ref[here, :], here)
        gy_ref[here, :] = gx
        grad_back(0, gx, step, chunk)

    loop(down, *DOWN)
    gwi_ref[1] = dot_rows(normed16[1], gproj[...]) * (1.0 / tokens)
    gwo_ref[0] = dot_rows(tnorm16[0], gh[...]) * (1.0 / tokens)

    triangle(tokens, tri, natural, side16.at[0], ga)
    triangle(tokens, tri, turned, flat16.at[0], gb)

    def last(step, chunk):
        grad_front(0, gy_ref[at_chunk(step, chunk), :], step, chunk)

    loop(last, *LAST)
    own = rows * tokens
    here = pl.ds(pl.multiple_of(row_id * own, own), own)
    gy_ref[here, :] = grad_state(0, gy_ref[here, :], here)
    gwi_ref[0] = dot_rows(normed16[0], gproj[...]) * (1.0 / tokens)

    c0 = pl.multiple_of((chan_id * n_sub + sub_id) * cols, TILE)
    for source, target in ((states.at[0], updated_ref), (gy_ref, pair_grad_ref)):
        for r in range(rows):
            at = pl.multiple_of((row_id * rows + r) * tokens + c0, TILE)
            target[r] = source[pl.ds(at, cols), :].astype(BF16)


def place(tokens, sizes, pieces, refs_in, x_ref, gy_ref):
    n_row, n_chan, n_sub = sizes
    row_id, chan_id, sub_id = lax.axis_index("row"), lax.axis_index("chan"), lax.axis_index("sub")
    rows, cols = tokens // n_row, tokens // (n_chan * n_sub)
    channels = x_ref.shape[-1]
    for ref, (row_steps, chan_step, sub_step) in zip(refs_in, pieces):
        chan, sub = jnp.bitwise_xor(chan_id, chan_step), jnp.bitwise_xor(sub_id, sub_step)
        c0 = (chan * n_sub + sub) * cols
        for k, row_step in enumerate(row_steps):
            row = jnp.bitwise_xor(row_id, row_step)
            for kind, target in ((0, x_ref), (1, gy_ref)):
                block = ref[k, kind].astype(F32).reshape(rows, cols, channels)
                for r in range(rows):
                    at = pl.multiple_of((row * rows + r) * tokens + c0, TILE)
                    target[pl.ds(at, cols), :] = block[r]


def from_step(block, axis, size, step):
    return lax.ppermute(block, axis, [(i, i ^ step) for i in range(size)])


def gather_part(pair, cotangent, sizes):
    n_row, n_chan, n_sub = sizes
    channels = pair.shape[-1]
    mine = jnp.stack([pair.reshape(-1, channels), cotangent.reshape(-1, channels)])
    row_steps = [0] + list(range(n_row - 1, 0, -1))
    column = jnp.stack([mine] + [from_step(mine, "row", n_row, step) for step in row_steps[1:]])
    parts = [column]
    pieces = [(row_steps, 0, 0)]
    cut = max(n_row // X_PARTS, 1)
    for chan_step in range(1, n_chan):
        for first in range(0, n_row, cut):
            parts.append(from_step(column[first : first + cut], "chan", n_chan, chan_step))
            pieces.append((row_steps[first : first + cut], chan_step, 0))
    for part, (steps, chan_step, _) in list(zip(parts, pieces)):
        for sub_step in range(1, n_sub):
            parts.append(from_step(part, "sub", n_sub, sub_step))
            pieces.append((steps, chan_step, sub_step))
    return parts, pieces


def whole_part(sizes, pair, cotangent, token_mask, w_in, w_out):
    tokens = token_mask.shape[0]
    channels = pair.shape[-1]
    hidden = w_out.shape[1]
    pairs = tokens * tokens
    parts, pieces = gather_part(pair, cotangent, sizes)
    plane = pltpu.VMEM((pairs, channels), F32)
    two = pltpu.VMEM((2, pairs, channels), F32)
    two16 = pltpu.VMEM((2, pairs, channels), BF16)
    plane16 = pltpu.VMEM((pairs, channels), BF16)
    vmem = pl.BlockSpec(memory_space=pltpu.VMEM)

    def kernel(*refs):
        count = len(parts)
        whole_kernel(tokens, sizes, pieces, refs[:count], *refs[count:])

    return pl.pallas_call(
        kernel,
        out_shape=(
            jax.ShapeDtypeStruct(pair.shape, BF16),
            jax.ShapeDtypeStruct(pair.shape, BF16),
            jax.ShapeDtypeStruct(w_in.shape, F32),
            jax.ShapeDtypeStruct(w_out.shape, F32),
        ),
        in_specs=[vmem] * len(parts) + [pl.BlockSpec(memory_space=pltpu.HBM)] * 3,
        out_specs=(vmem,) * 4,
        scratch_shapes=[
            two, plane, two, two, two16, two16, two, two, two16, two, two, two, two,
            two, two, two, two16, two, plane, plane16, plane16, plane, plane,
            pltpu.VMEM(w_in.shape, BF16),
            pltpu.VMEM((2, w_in.shape[2], channels), BF16),
            pltpu.VMEM((2, channels, hidden), BF16),
            pltpu.VMEM((pairs, w_in.shape[2]), BF16),
            pltpu.VMEM((pairs, channels), BF16),
            pltpu.VMEM((tokens, channels), F32),
            pltpu.SMEM((tokens,), jnp.int32),
            pltpu.VMEM(w_in.shape, BF16),
            pltpu.VMEM(w_out.shape, BF16),
            pltpu.SemaphoreType.DMA((3,)),
        ],
        compiler_params=pltpu.CompilerParams(vmem_limit_bytes=VMEM_BYTES),
    )(*parts, token_mask, w_in, w_out)


def layer_norm(values, norm_axis):
    centre = jnp.mean(values, axis=norm_axis, keepdims=True)
    shifted = values - centre
    spread = jnp.mean(shifted * shifted, axis=norm_axis, keepdims=True)
    inverse = lax.rsqrt(spread + EPSILON)
    return (shifted * inverse, inverse)


def norm_grad(upstream, normed, inverse, norm_axis):
    return inverse * (
        upstream
        - jnp.mean(upstream, axis=norm_axis, keepdims=True)
        - normed * jnp.mean(upstream * normed, axis=norm_axis, keepdims=True)
    )


def product_of(pattern, left_op, right_op):
    return jnp.einsum(pattern, left_op, right_op, preferred_element_type=jnp.float32)


def split_weights(w_in_u, hidden):
    channels = w_in_u.shape[0]
    return (w_in_u[:, : 4 * hidden].reshape(channels, 4, hidden), w_in_u[:, 4 * hidden :])


def front_block(state_block, rows_mask, cols_mask, w_in_u, hidden):
    normed, _ = layer_norm(state_block.astype(jnp.float32), -1)
    normed = normed.astype(jnp.bfloat16)
    w_pairs, w_gate = split_weights(w_in_u, hidden)
    projected = product_of("rjc,cke->kerj", normed, w_pairs)
    pair_mask = rows_mask[:, None] * cols_mask[None, :]
    left_side = jax.nn.sigmoid(projected[1]) * projected[0] * pair_mask
    right_side = jax.nn.sigmoid(projected[3]) * projected[2] * pair_mask
    return jnp.stack([left_side, right_side]).astype(jnp.bfloat16)


def back_block(state_block, tri_block, w_in_u, w_out_u, hidden):
    normed, _ = layer_norm(state_block.astype(jnp.float32), -1)
    normed = normed.astype(jnp.bfloat16)
    _, w_gate = split_weights(w_in_u, hidden)
    gate_value = jax.nn.sigmoid(product_of("rjc,cd->rjd", normed, w_gate))
    tnorm, _ = layer_norm(tri_block.astype(jnp.float32), 0)
    linear = product_of("erj,ec->rjc", tnorm.astype(jnp.bfloat16), w_out_u)
    return (state_block.astype(jnp.float32) + gate_value * linear).astype(jnp.bfloat16)


def grad_back_block(state_block, tri_block, upstream, w_in_u, w_out_u, hidden):
    normed, _ = layer_norm(state_block.astype(jnp.float32), -1)
    normed = normed.astype(jnp.bfloat16)
    _, w_gate = split_weights(w_in_u, hidden)
    gate_value = jax.nn.sigmoid(product_of("rjc,cd->rjd", normed, w_gate))
    tnorm, inverse = layer_norm(tri_block.astype(jnp.float32), 0)
    tnorm_low = tnorm.astype(jnp.bfloat16)
    grad_hidden = (upstream * gate_value).astype(jnp.bfloat16)
    wo_term = product_of("erj,rjc->ec", tnorm_low, grad_hidden)
    grad_tn = product_of("rjc,ec->erj", grad_hidden, w_out_u)
    grad_tri = norm_grad(grad_tn, tnorm, inverse, 0).astype(jnp.bfloat16)
    return (grad_tri, wo_term)


def grad_front_block(
    state_block, tri_block, grad_pairs, upstream, rows_mask, cols_mask, w_in_u, w_out_u, hidden
):
    normed_full, inverse = layer_norm(state_block.astype(jnp.float32), -1)
    normed = normed_full.astype(jnp.bfloat16)
    w_pairs, w_gate = split_weights(w_in_u, hidden)
    projected = product_of("rjc,cke->kerj", normed, w_pairs)
    gate_value = jax.nn.sigmoid(product_of("rjc,cd->rjd", normed, w_gate))
    tnorm, _ = layer_norm(tri_block.astype(jnp.float32), 0)
    linear = product_of("erj,ec->rjc", tnorm.astype(jnp.bfloat16), w_out_u)
    grad_gate = (upstream * linear * gate_value * (1.0 - gate_value)).astype(jnp.bfloat16)
    pair_mask = rows_mask[:, None] * cols_mask[None, :]
    sig_left = jax.nn.sigmoid(projected[1])
    sig_right = jax.nn.sigmoid(projected[3])
    grad_left = grad_pairs[0].astype(jnp.float32) * pair_mask
    grad_right = grad_pairs[1].astype(jnp.float32) * pair_mask
    grad_proj = jnp.stack(
        [
            grad_left * sig_left,
            grad_left * projected[0] * sig_left * (1.0 - sig_left),
            grad_right * sig_right,
            grad_right * projected[2] * sig_right * (1.0 - sig_right),
        ]
    ).astype(jnp.bfloat16)
    channels = state_block.shape[2]
    pair_term = product_of("rjc,kerj->cke", normed, grad_proj).reshape(channels, 4 * hidden)
    gate_term = product_of("rjc,rjd->cd", normed, grad_gate)
    wi_term = jnp.concatenate([pair_term, gate_term], axis=1)
    grad_normed = product_of("kerj,cke->rjc", grad_proj, w_pairs) + product_of(
        "rjd,cd->rjc", grad_gate, w_gate
    )
    grad_x = upstream + norm_grad(grad_normed, normed_full, inverse, -1)
    return (grad_x, wi_term)


def to_channels(stacked):
    return lax.all_to_all(stacked, ("chan", "sub"), split_axis=1, concat_axis=3, tiled=True)


def to_columns(stacked):
    return lax.all_to_all(stacked, ("chan", "sub"), split_axis=3, concat_axis=1, tiled=True)


def turn_rows(matrix):
    return lax.all_to_all(matrix, "row", split_axis=2, concat_axis=1, tiled=True)


def fold_rows(source, folder, initial):
    return folder(initial, lax.all_gather(source, "row", axis=1, tiled=True), jnp.int32(0))


def spread_part(pair, cotangent, token_mask, w_in, w_out):
    row_count, col_count, _ = pair.shape
    hidden = w_out.shape[1]
    token_total = token_mask.shape[0]
    row_id = lax.axis_index("row")
    col_id = lax.axis_index(("chan", "sub"))
    mask_full = token_mask.astype(jnp.float32)
    rows_mask = lax.dynamic_slice_in_dim(mask_full, row_id * row_count, row_count)
    cols_mask = lax.dynamic_slice_in_dim(mask_full, col_id * col_count, col_count)
    states = [pair]
    saved = []
    for layer_id in range(2):
        current = states[-1]
        pairs_local = front_block(current, rows_mask, cols_mask, w_in[layer_id], hidden)
        spread = to_channels(pairs_local)
        left_rows = spread[0]
        right_rows = spread[1]
        zero_tri = jnp.zeros(left_rows.shape, jnp.float32)
        keeper = None
        if layer_id == 0:

            def out_forward(totals, portion, offset):
                product_block = product_of("qrk,qjk->qrj", left_rows, portion)
                return product_block

            tri_rows = fold_rows(right_rows, out_forward, zero_tri)
        else:
            left_turned = turn_rows(left_rows)

            def in_forward(totals, portion, offset):
                return product_of("qki,qkj->qij", left_turned, portion)

            tri_rows = fold_rows(right_rows, in_forward, zero_tri)
        tri_cols = to_columns(tri_rows.astype(jnp.bfloat16)[None])[0]
        states.append(back_block(current, tri_cols, w_in[layer_id], w_out[layer_id], hidden))
        saved.append((left_rows, right_rows, tri_cols, keeper))
    upstream = cotangent.astype(jnp.float32)
    wi_grads = [None, None]
    wo_grads = [None, None]
    for layer_id in (1, 0):
        left_rows, right_rows, tri_cols, keeper = saved[layer_id]
        current = states[layer_id]
        grad_tri, wo_term = grad_back_block(
            current, tri_cols, upstream, w_in[layer_id], w_out[layer_id], hidden
        )
        grad_rows = to_channels(grad_tri[None])[0]
        zero_grad = jnp.zeros(left_rows.shape, jnp.float32)
        if layer_id == 1:

            def in_backward(carried, portion, offset):
                left_block = product_of("qkj,qij->qki", right_rows, portion)
                return (left_block, product_of("qki,qij->qkj", left_rows, portion))

            grad_left, grad_right = fold_rows(grad_rows, in_backward, (zero_grad, zero_grad))
        else:
            grad_turned = turn_rows(grad_rows)

            def right_step(totals, portion, offset):
                return product_of("qij,qik->qjk", grad_turned, portion)

            def left_step(totals, portion, offset):
                return product_of("qij,qjk->qik", grad_rows, portion)

            grad_left = fold_rows(right_rows, left_step, zero_grad)
            grad_right = fold_rows(left_rows, right_step, zero_grad)
        grad_pairs = to_columns(jnp.stack([grad_left, grad_right]).astype(jnp.bfloat16))
        upstream, wi_term = grad_front_block(
            current,
            tri_cols,
            grad_pairs,
            upstream,
            rows_mask,
            cols_mask,
            w_in[layer_id],
            w_out[layer_id],
            hidden,
        )
        wi_grads[layer_id] = wi_term
        wo_grads[layer_id] = wo_term
    wi_sum, wo_sum = lax.psum((jnp.stack(wi_grads), jnp.stack(wo_grads)), ("row", "chan", "sub"))
    return (states[2], upstream.astype(jnp.bfloat16), wi_sum / token_total, wo_sum / token_total)


def solution(mesh):
    sizes = tuple(mesh.shape[axis] for axis in ("row", "chan", "sub"))

    def shards(pair, cotangent, token_mask, w_in, w_out):
        tokens = token_mask.shape[0]
        tiled = tokens % (TILE * sizes[1] * sizes[2]) == 0
        tiled = tiled and all(size & (size - 1) == 0 for size in sizes)
        if tiled and PLANES * tokens * tokens * pair.shape[-1] * 4 <= VMEM_PLAN:
            return whole_part(sizes, pair, cotangent, token_mask, w_in, w_out)
        return spread_part(pair, cotangent, token_mask, w_in, w_out)

    placed = (
        P(("groups", "row"), ("chan", "sub"), None),
        P(("groups", "row"), ("chan", "sub"), None),
        P("groups"),
        P(),
        P(),
    )
    return jax.shard_map(
        shards,
        mesh=mesh,
        in_specs=placed,
        out_specs=(
            P(("groups", "row"), ("chan", "sub"), None),
            P(("groups", "row"), ("chan", "sub"), None),
            P("groups", None, None),
            P("groups", None, None),
        ),
        check_vma=False,
    )
```
